128 devices in a mesh: ctx: 32 (over x, y, core), tp: 4 (over z).
Axes of the slice: x: 4, y: 4, z: 4, core: 2. Of those that a mesh axis runs over, the one named last changes fastest.
Arguments:
- queries: bfloat16 [32768, 8192], P(('ctx', 'tp')), may hold values from -36 to 36
- key_rows: bfloat16 [32768, 1024], P(('ctx', 'tp')), may hold values from -6 to 6
- value_rows: bfloat16 [32768, 1024], P(('ctx', 'tp')), may hold values from -6 to 6
- vertical_keys: int32 [8, 1024], P('tp'), may hold values from 0 to 32767, as said below
- slash_offsets: int32 [8, 3], P('tp'), may hold values from 0 to 32704, as said below
Outputs:
- attended: bfloat16 [32768, 8192], P('ctx', 'tp')
The draws below stay inside these ranges and needn't reach their ends.
Inputs may be any that keep to these rules, and one draw needn't show every extreme that they name: `vertical_keys`: each row holds 1024 distinct positions in ascending order; no more than 96 of a row lie in one aligned range of 1024 positions, and in every row some such range holds exactly 96. `slash_offsets`: each row holds 3 distinct multiples of 64, the first of them 0.
All inputs are finite; a program needn't handle non-finite values.
Results may differ from the reference program's by a relative error of at most 0.0035.
Values may be sent and summed in bfloat16 or wider, within the bound.
No kernel may reach another device: no remote copies, remote signals or barrier semaphores. Data moves between devices by JAX's collectives and lax.ppermute only.
A program may use at most 320 MiB of HBM per device.

```python
import jax
import jax.numpy as jnp
from jax import lax

HQ = 64
KVH = 8
DH = 128
TOK_DEV = 1024
NVERT = 1024
NBAND = 3
TOKENS = 32768
CAP = 96


def draw_queries(key, part):
    key = jax.random.fold_in(key, 1)
    group_size = HQ // KVH
    base_field = 2.0 * jnp.clip(jax.random.normal(key, (TOKENS, KVH, group_size, DH), jnp.float32), -6.0, 6.0)
    return base_field.reshape(TOKENS, HQ * DH).astype(jnp.bfloat16)


def draw_key_rows(key, part):
    key = jax.random.fold_in(key, 2)
    base_field = jnp.clip(jax.random.normal(key, (TOKENS, KVH, DH), jnp.float32), -6.0, 6.0)
    return base_field.reshape(TOKENS, KVH * DH).astype(jnp.bfloat16)


def draw_vertical_keys(key, part):
    key = jax.random.fold_in(key, 21)
    shards = TOKENS // TOK_DEV
    remaining = NVERT - CAP
    spread = remaining // (shards - 1)
    leftover = remaining % (shards - 1)

    def one_head(head_key):
        first_key, second_key, third_key = jax.random.split(head_key, 3)
        heavy = jax.random.randint(first_key, (), 0, shards)
        jitter = jax.random.randint(second_key, (shards - 1,), 0, spread // 2 + 1)
        order = jnp.arange(shards - 1)
        others = spread + (order < leftover).astype(jnp.int32) + jitter - jnp.roll(jitter, -1)
        slots = jnp.arange(shards)
        lowered = jnp.clip(slots - (slots > heavy).astype(jnp.int32), 0, shards - 2)
        counts = jnp.where(slots == heavy, CAP, others[lowered])
        ranks = jax.vmap(lambda shard_key: jax.random.permutation(shard_key, TOK_DEV))(jax.random.split(third_key, shards))
        chosen = (ranks < counts[:, None]).reshape(TOKENS)
        return jnp.nonzero(chosen, size=NVERT)[0].astype(jnp.int32)
    return jax.vmap(one_head)(jax.random.split(key, KVH))


def draw_slash_offsets(key, part):
    key = jax.random.fold_in(key, 31)
    spots = TOKENS // 64
    first_key, second_key = jax.random.split(key)

    def one_head(head_key):
        return jax.random.permutation(head_key, spots - 2)[:NBAND - 1] + 1
    picks = jax.vmap(one_head)(jax.random.split(first_key, KVH))
    far_head = jax.random.randint(second_key, (), 0, KVH)
    first_col = jnp.where(jnp.arange(KVH) == far_head, spots - 1, picks[:, 0])
    picks = picks.at[:, 0].set(first_col)
    offsets = jnp.concatenate((jnp.zeros((KVH, 1), jnp.int32), picks.astype(jnp.int32)), axis=1)
    return (64 * offsets).astype(jnp.int32)


def block_levels(own_key, shape, cuts, low, high):
    loudness, own = 1.0, jax.random.fold_in(own_key, 6)
    for position, parts in cuts:
        heights = jnp.exp(jax.random.uniform(jax.random.fold_in(own, position), (parts,), jnp.float32, low / len(cuts), high / len(cuts)))
        loudness = loudness * jnp.repeat(heights, shape[position] // parts).reshape([-1 if axis == position else 1 for axis in range(len(shape))])
    return loudness


def bell_draw(stream_key, dims, deviation, most, cuts=(), held_as=jnp.bfloat16):
    loudness = block_levels(stream_key, dims, cuts, -0.22, 0.18) if cuts else 1.0
    array = jax.random.normal(stream_key, dims, jnp.float32) * deviation * loudness
    return jnp.minimum(jnp.maximum(array, -most), most).astype(held_as)


def setup_inputs(seed: int = 0) -> dict:
    keys = jax.random.split(jax.random.key(seed), 6)
    return {
        "queries": draw_queries(jax.random.fold_in(keys[5], 71), 0),
        "key_rows": draw_key_rows(jax.random.fold_in(keys[5], 71), 0),
        "value_rows": bell_draw(keys[2], (TOKENS, KVH * DH), 1.0, 6.0, ((0, 128),)),
        "vertical_keys": draw_vertical_keys(jax.random.fold_in(keys[5], 71), 0),
        "slash_offsets": draw_slash_offsets(jax.random.fold_in(keys[5], 71), 0),
    }


def reference(queries, key_rows, value_rows, vertical_keys, slash_offsets):
    group_size = HQ // KVH
    scale_factor = DH ** -0.5
    key_heads = key_rows.reshape(TOKENS, KVH, DH).transpose(1, 0, 2)
    value_heads = value_rows.reshape(TOKENS, KVH, DH).transpose(1, 0, 2)
    head_ids = jnp.arange(KVH, dtype=jnp.int32)[:, None]
    vert_k = key_heads[head_ids, vertical_keys].astype(jnp.float32)
    vert_v = value_heads[head_ids, vertical_keys].astype(jnp.float32)
    marked = jnp.zeros((KVH, TOKENS), jnp.int32).at[head_ids, vertical_keys].set(1)
    marked_pad = jnp.concatenate((jnp.zeros_like(marked), marked), axis=1)
    pad_zero = jnp.zeros((KVH, TOKENS, DH), jnp.bfloat16)
    key_pad = jnp.concatenate((pad_zero, key_heads), axis=1)
    value_pad = jnp.concatenate((pad_zero, value_heads), axis=1)
    distance = jnp.arange(192, dtype=jnp.int32)[None, :] - jnp.arange(128, dtype=jnp.int32)[:, None]
    in_band = (distance >= 1) & (distance <= 64)

    def cut_tiles(table, firsts):
        return jax.vmap(lambda begin: lax.dynamic_slice_in_dim(table, begin + TOKENS, 192, 0))(firsts)

    def one_block(block_id):
        first_row = block_id * 128
        query_block = lax.dynamic_slice_in_dim(queries, first_row, 128, 0)
        query_block = query_block.reshape(128, KVH, group_size, DH).astype(jnp.float32)
        positions = first_row + jnp.arange(128, dtype=jnp.int32)
        vert_scores = jnp.einsum("qhgd,hnd->hgqn", query_block, vert_k) * scale_factor
        vert_mask = vertical_keys[:, None, None, :] <= positions[None, None, :, None]
        vert_scores = jnp.where(vert_mask, vert_scores, -jnp.inf)
        tile_first = (first_row - slash_offsets - 64).astype(jnp.int32)
        band_k = jax.vmap(cut_tiles)(key_pad, tile_first).astype(jnp.float32)
        band_v = jax.vmap(cut_tiles)(value_pad, tile_first).astype(jnp.float32)
        band_marks = jax.vmap(cut_tiles)(marked_pad, tile_first)
        band_pos = tile_first[:, :, None] + jnp.arange(192, dtype=jnp.int32)[None, None, :]
        band_ok = (band_pos >= 0) & (band_marks == 0)
        band_scores = jnp.einsum("qhgd,hktd->hgqkt", query_block, band_k) * scale_factor
        band_mask = in_band[None, None, :, None, :] & band_ok[:, None, None, :, :]
        band_scores = jnp.where(band_mask, band_scores, -jnp.inf)
        top = jnp.maximum(jnp.max(vert_scores, axis=-1), jnp.max(band_scores, axis=(-2, -1)))
        vert_weight = jnp.exp(vert_scores - top[..., None])
        band_weight = jnp.exp(band_scores - top[..., None, None])
        total = jnp.sum(vert_weight, axis=-1) + jnp.sum(band_weight, axis=(-2, -1))
        vert_round = lax.optimization_barrier(vert_weight.astype(jnp.bfloat16)).astype(jnp.float32)
        band_round = lax.optimization_barrier(band_weight.astype(jnp.bfloat16)).astype(jnp.float32)
        numer = jnp.einsum("hgqn,hnd->hgqd", vert_round, vert_v)
        numer = numer + jnp.einsum("hgqkt,hktd->hgqd", band_round, band_v)
        result = numer / total[..., None]
        return result.transpose(2, 0, 1, 3).reshape(128, HQ * DH).astype(jnp.bfloat16)

    blocks = lax.map(one_block, jnp.arange(TOKENS // 128, dtype=jnp.int32))
    return blocks.reshape(TOKENS, HQ * DH)
```

```python
import functools

import jax
import jax.numpy as jnp
from jax import lax
from jax.experimental import pallas as pl
from jax.experimental.pallas import tpu as pltpu
from jax.sharding import PartitionSpec as P

HQ = 64
KVH = 8
DH = 128
NVERT = 1024
GROUP = HQ // KVH
BLOCK = 64
CAP = 96
NX, NY, NCORE, NTP = 4, 4, 2, 4
NCTX = NX * NY * NCORE
TOK = 1024
NBLK = TOK // BLOCK
PIECE = TOK // NTP
LOG2_SCALE = 1.4426950408889634 * DH**-0.5
NEG = -1e30
BF16 = jnp.bfloat16
F32 = jnp.float32
VMEM_LIMIT = 56 * 2**20


def params():
    return pltpu.CompilerParams(vmem_limit_bytes=VMEM_LIMIT)


def dot_t(left, right):
    return lax.dot_general(left, right, (((1,), (1,)), ((), ())), preferred_element_type=F32)


def tp_shift(block, distance):
    return lax.ppermute(block, "tp", [(i, (i + distance) % NTP) for i in range(NTP)])


def ctx_route(block, move):
    pairs = []
    for x in range(NX):
        for y in range(NY):
            for core in range(NCORE):
                to_x, to_y, to_core = move(x, y, core)
                source = (x * NY + y) * NCORE + core
                target = ((to_x % NX) * NY + to_y % NY) * NCORE + to_core % NCORE
                pairs.append((source, target))
    return lax.ppermute(block, "ctx", pairs)


def ctx_next(block):
    return lax.ppermute(block, "ctx", [(i, i + 1) for i in range(NCTX - 1)])


def join_kernel(rows_ref, keys_ref, p0, p1, p2, p3, out_ref, own_ref):
    for distance, piece in enumerate((p0, p1, p2, p3)):
        first = pl.multiple_of(rows_ref[distance] * PIECE, PIECE)
        out_ref[:, pl.ds(first, PIECE), :] = piece[...]
    spots = lax.broadcasted_iota(jnp.int32, (CAP, TOK), 1)
    for head in range(2):
        chosen = jnp.where(keys_ref[head] == spots, 1.0, 0.0).astype(BF16)
        own_ref[head] = jnp.dot(chosen, out_ref[head], preferred_element_type=F32).astype(BF16)


def join_pieces(rows, own_keys, pieces):
    vmem = pl.BlockSpec(memory_space=pltpu.VMEM)
    return pl.pallas_call(
        join_kernel,
        in_specs=[pl.BlockSpec(memory_space=pltpu.SMEM)] + [vmem] * 5,
        out_specs=[vmem, vmem],
        out_shape=[
            jax.ShapeDtypeStruct((2, TOK, 2 * DH), BF16),
            jax.ShapeDtypeStruct((2, CAP, 2 * DH), BF16),
        ],
        compiler_params=params(),
    )(rows, own_keys, *pieces)


def spread_kernel(shift_ref, table_ref, out_ref):
    group = pl.program_id(0)
    for i in range(8):
        for band in range(2):
            source = jnp.maximum(group * 8 + i - shift_ref[band], 0)
            out_ref[i, band] = table_ref[source]


def spread_windows(shifts, table):
    return pl.pallas_call(
        spread_kernel,
        grid_spec=pltpu.PrefetchScalarGridSpec(
            num_scalar_prefetch=1,
            grid=(NCTX // 8,),
            in_specs=[pl.BlockSpec((NCTX, BLOCK, 2 * DH), lambda g, s: (0, 0, 0))],
            out_specs=pl.BlockSpec((8, 2, BLOCK, 2 * DH), lambda g, s: (g, 0, 0, 0)),
        ),
        out_shape=jax.ShapeDtypeStruct((NCTX, 2, BLOCK, 2 * DH), BF16),
        compiler_params=params(),
    )(shifts, table)


def close_kernel(first_ref, *refs):
    sources, out_ref, total = refs[:8], refs[8], refs[9]
    head = pl.program_id(0)
    total[...] = jnp.zeros_like(total)
    for number, source in enumerate(sources):
        for i in range(4):
            first = first_ref[head, number * 4 + i]
            for half in range(2):
                columns = slice(half * DH, (half + 1) * DH)
                total[half, pl.ds(first, CAP), :] += source[i, 0, :, columns].astype(F32)
    for half in range(2):
        out_ref[0, :, half * DH : (half + 1) * DH] = total[half, :NVERT, :].astype(BF16)
    out_ref[0, :, 2 * DH :] = jnp.ones((NVERT, DH), BF16)


def close_up(firsts, gathered):
    return pl.pallas_call(
        close_kernel,
        grid_spec=pltpu.PrefetchScalarGridSpec(
            num_scalar_prefetch=1,
            grid=(2,),
            in_specs=[pl.BlockSpec((4, 1, CAP, 2 * DH), lambda h, s: (0, h, 0, 0))] * 8,
            out_specs=pl.BlockSpec((1, NVERT, 3 * DH), lambda h, s: (h, 0, 0)),
            scratch_shapes=[pltpu.VMEM((2, NVERT + CAP + 8, DH), F32)],
        ),
        out_shape=jax.ShapeDtypeStruct((2, NVERT, 3 * DH), BF16),
        compiler_params=params(),
    )(firsts, *gathered)


def stack_heads(ref, first):
    return jnp.concatenate(
        [ref[first : first + BLOCK, g * DH : (g + 1) * DH] for g in range(GROUP)], axis=0
    )


def band_bias():
    row = lax.broadcasted_iota(jnp.int32, (BLOCK, 2 * BLOCK), 0)
    column = lax.broadcasted_iota(jnp.int32, (BLOCK, 2 * BLOCK), 1)
    distance = row - column + BLOCK
    return jnp.where((distance >= 0) & (distance < BLOCK), 0.0, NEG)


def masked(scores, bias):
    width = scores.shape[1]
    return (scores.reshape(GROUP, BLOCK, width) + bias[None]).reshape(GROUP * BLOCK, width)


def near_kernel(piece_ref, q_ref, vert_ref, near_ref, spot_ref, mark_ref, *refs):
    out_ref, stat_ref, copy_ref = refs[-3:]
    tile = pl.program_id(1)
    ones = jnp.ones((2 * BLOCK, DH), BF16)
    lanes = lax.broadcasted_iota(jnp.int32, (BLOCK, DH), 1)
    bias = band_bias()
    copy_ref[...] = q_ref[...]
    subtiles = q_ref.shape[0] // BLOCK
    for sub in range(subtiles):
        block = piece_ref[0] * (PIECE // BLOCK) + tile * subtiles + sub
        query = stack_heads(q_ref, sub * BLOCK)
        near = near_ref[0, pl.ds(pl.multiple_of(block * BLOCK, BLOCK), 2 * BLOCK), :]
        position = block * BLOCK + lax.broadcasted_iota(jnp.int32, (BLOCK, NVERT), 0)
        vert_bias = jnp.where(spot_ref[0] <= position, 0.0, NEG)
        near_bias = bias + mark_ref[0, 0, pl.ds(block, 1), :]
        vert_s = masked(dot_t(query, vert_ref[0, :, :DH]), vert_bias)
        near_s = masked(dot_t(query, near[:, :DH]), near_bias)
        top = jnp.maximum(
            jnp.max(vert_s, axis=-1, keepdims=True), jnp.max(near_s, axis=-1, keepdims=True)
        )
        top = top * LOG2_SCALE
        vert_w = jnp.exp2(vert_s * LOG2_SCALE - top).astype(BF16)
        near_w = jnp.exp2(near_s * LOG2_SCALE - top).astype(BF16)
        both = jnp.dot(vert_w, vert_ref[0, :, DH:], preferred_element_type=F32)
        both = both + jnp.dot(
            near_w, jnp.concatenate([near[:, DH:], ones], axis=1), preferred_element_type=F32
        )
        total = both[:, DH:]
        out = both[:, :DH] / total
        level = top + jnp.log2(total)
        stat = jnp.zeros((BLOCK, DH), F32)
        for g in range(GROUP):
            rows = slice(g * BLOCK, (g + 1) * BLOCK)
            out_ref[sub * BLOCK : (sub + 1) * BLOCK, g * DH : (g + 1) * DH] = out[rows]
            stat = jnp.where(lanes == g, level[rows], stat)
        stat_ref[sub * BLOCK : (sub + 1) * BLOCK, :] = stat


def near_attention(piece, query, vert, near, spots, marks, state):
    tile = 128
    tiles = PIECE // tile
    wide = GROUP * DH
    at_piece = lambda h, t, s: (s[0] * tiles + t, h)
    shapes = [
        jax.ShapeDtypeStruct((TOK, 2 * wide), F32),
        jax.ShapeDtypeStruct((TOK, 2 * DH), F32),
        jax.ShapeDtypeStruct((TOK, 2 * wide), BF16),
    ]
    state_specs = [pl.BlockSpec(memory_space=pl.ANY)] * len(state)
    rows = PIECE * 2 * GROUP
    return pl.pallas_call(
        near_kernel,
        grid_spec=pltpu.PrefetchScalarGridSpec(
            num_scalar_prefetch=1,
            grid=(2, tiles),
            in_specs=[
                pl.BlockSpec((tile, wide), lambda h, t, s: (t, h)),
                pl.BlockSpec((1, NVERT, 3 * DH), lambda h, t, s: (h, 0, 0)),
                pl.BlockSpec((1, TOK + BLOCK, 2 * DH), lambda h, t, s: (h, 0, 0)),
                pl.BlockSpec((1, 1, NVERT), lambda h, t, s: (h, 0, 0)),
                pl.BlockSpec((1, 1, NBLK, 2 * BLOCK), lambda h, t, s: (h, 0, 0, 0)),
            ]
            + state_specs,
            out_specs=[
                pl.BlockSpec((tile, wide), at_piece),
                pl.BlockSpec((tile, DH), at_piece),
                pl.BlockSpec((tile, wide), at_piece),
            ],
        ),
        out_shape=shapes,
        input_output_aliases={6 + i: i for i in range(len(state))},
        cost_estimate=pl.CostEstimate(
            flops=rows * (NVERT + 2 * BLOCK) * 4 * 2 * DH,
            bytes_accessed=8 * 2**20,
            transcendentals=rows * (NVERT + 2 * BLOCK),
        ),
        compiler_params=params(),
    )(piece, query, vert, near, spots, marks, *state)


def far_kernel(order_ref, q_ref, prior_ref, stat_ref, far_ref, halo_ref, mark_ref, out_ref, keys):
    head = pl.program_id(0)
    tile = pl.program_id(1)

    @pl.when(tile == 0)
    def _():
        for band in range(2):
            keys[band, :BLOCK, :] = halo_ref[0, band]
            for block in range(NBLK):
                source = lax.rem(block + NBLK - order_ref[head * 2 + band], NBLK)
                keys[band, (block + 1) * BLOCK : (block + 2) * BLOCK, :] = far_ref[0, source, band]

    ones = jnp.ones((4 * BLOCK, DH), BF16)
    bias = band_bias()
    subtiles = q_ref.shape[0] // BLOCK
    for sub in range(subtiles):
        block = tile * subtiles + sub
        first = pl.multiple_of(block * BLOCK, BLOCK)
        query = stack_heads(q_ref, sub * BLOCK)
        near = jnp.concatenate([keys[band, pl.ds(first, 2 * BLOCK), :] for band in range(2)], axis=0)
        both_bias = jnp.concatenate(
            [bias + mark_ref[0, 1 + band, pl.ds(block, 1), :] for band in range(2)], axis=1
        )
        scores = masked(dot_t(query, near[:, :DH]), both_bias)
        stat = stat_ref[sub * BLOCK : (sub + 1) * BLOCK, :]
        level = jnp.concatenate([stat[:, g : g + 1] for g in range(GROUP)], axis=0)
        top = jnp.maximum(jnp.max(scores, axis=-1, keepdims=True) * LOG2_SCALE, level)
        weight = jnp.exp2(scores * LOG2_SCALE - top).astype(BF16)
        both = jnp.dot(
            weight, jnp.concatenate([near[:, DH:], ones], axis=1), preferred_element_type=F32
        )
        prior_w = jnp.exp2(level - top)
        total = both[:, DH:] + prior_w
        prior = jnp.concatenate(
            [
                prior_ref[sub * BLOCK : (sub + 1) * BLOCK, g * DH : (g + 1) * DH]
                for g in range(GROUP)
            ],
            axis=0,
        )
        out = ((both[:, :DH] + prior * prior_w) / total).astype(BF16)
        for g in range(GROUP):
            out_ref[sub * BLOCK : (sub + 1) * BLOCK, g * DH : (g + 1) * DH] = out[
                g * BLOCK : (g + 1) * BLOCK
            ]


def far_attention(orders, query, prior, stats, far, halo, marks):
    tile = 128
    wide = GROUP * DH
    rows = TOK * 2 * GROUP
    return pl.pallas_call(
        far_kernel,
        grid_spec=pltpu.PrefetchScalarGridSpec(
            num_scalar_prefetch=1,
            grid=(2, TOK // tile),
            in_specs=[
                pl.BlockSpec((tile, wide), lambda h, t, s: (t, h)),
                pl.BlockSpec((tile, wide), lambda h, t, s: (t, h)),
                pl.BlockSpec((tile, DH), lambda h, t, s: (t, h)),
                pl.BlockSpec((1, NBLK, 2, BLOCK, 2 * DH), lambda h, t, s: (h, 0, 0, 0, 0)),
                pl.BlockSpec((1, 2, BLOCK, 2 * DH), lambda h, t, s: (h, 0, 0, 0)),
                pl.BlockSpec((1, 3, NBLK, 2 * BLOCK), lambda h, t, s: (h, 0, 0, 0)),
            ],
            out_specs=pl.BlockSpec((tile, wide), lambda h, t, s: (t, h)),
            scratch_shapes=[pltpu.VMEM((2, TOK + BLOCK, 2 * DH), BF16)],
        ),
        out_shape=jax.ShapeDtypeStruct((TOK, 2 * wide), BF16),
        cost_estimate=pl.CostEstimate(
            flops=rows * 4 * BLOCK * 4 * 2 * DH,
            bytes_accessed=20 * 2**20,
            transcendentals=rows * 4 * BLOCK,
        ),
        compiler_params=params(),
    )(orders, query, prior, stats, far, halo, marks)


def shards(queries, key_rows, value_rows, vertical_keys, slash_offsets):
    tp = lax.axis_index("tp")
    ctx = lax.axis_index("ctx")
    base = ctx * TOK
    heads = vertical_keys.shape[0]

    kv = jnp.concatenate(
        (key_rows.reshape(PIECE, KVH, DH), value_rows.reshape(PIECE, KVH, DH)), axis=2
    ).transpose(1, 0, 2)
    kv_pieces = []
    for distance in range(NTP):
        part = lax.dynamic_slice_in_dim(kv, heads * ((tp + distance) % NTP), heads, 0)
        kv_pieces.append(tp_shift(part, distance) if distance else part)
    kv_pieces[1:], queries = lax.optimization_barrier((kv_pieces[1:], queries))

    first_own = jnp.sum(vertical_keys < base, axis=1)
    own_count = jnp.sum(vertical_keys < base + TOK, axis=1) - first_own
    extended = jnp.concatenate((vertical_keys, jnp.zeros((heads, CAP), jnp.int32)), axis=1)
    own_keys = jnp.stack(
        [lax.dynamic_slice_in_dim(extended[h], first_own[h], CAP, 0) for h in range(heads)]
    )
    live = jnp.arange(CAP, dtype=jnp.int32)[None, :] < own_count[:, None]
    own_keys = jnp.where(live, own_keys - base, -1)
    piece_rows = (tp + NTP - jnp.arange(NTP, dtype=jnp.int32)) % NTP
    local, own = join_pieces(piece_rows, own_keys[:, :, None], kv_pieces)

    table = lax.all_to_all(
        local.reshape(NCTX, BLOCK, 2 * DH), "ctx", split_axis=0, concat_axis=0, tiled=True
    )

    q_pieces = []
    for distance in range(NTP):
        wide = queries.shape[1] // NTP
        part = lax.dynamic_slice_in_dim(queries, wide * ((tp + distance) % NTP), wide, 1)
        q_pieces.append(tp_shift(part, distance) if distance else part)

    along_y = [own]
    for step in (1, 2, 3):
        along_y.append(ctx_route(own, lambda x, y, core, step=step: (x, y + step, core)))
    along_y = jnp.stack(along_y)
    along_x = [along_y]
    for step in (1, 2, 3):
        along_x.append(ctx_route(along_y, lambda x, y, core, step=step: (x + step, y, core)))
    across = [ctx_route(part, lambda x, y, core: (x, y, core + 1)) for part in along_x]
    slots = jnp.arange(NCTX, dtype=jnp.int32)
    slot_core, slot_x, slot_y = slots // 16, (slots // 4) % 4, slots % 4
    x, y, core = ctx // 8, (ctx // 2) % 4, ctx % 2
    owners = ((x + 4 - slot_x) % 4) * 8 + ((y + 4 - slot_y) % 4) * 2 + (core + slot_core) % 2
    firsts = jnp.sum(
        vertical_keys[:, None, :] < (owners * TOK)[None, :, None], axis=2, dtype=jnp.int32
    )
    vert = close_up(firsts, along_x + across)

    high = (vertical_keys[:, :, None] // BLOCK == jnp.arange(NCTX * NBLK)).astype(BF16)
    low = (vertical_keys[:, :, None] % BLOCK == jnp.arange(BLOCK)).astype(BF16)
    marked = jnp.einsum("hnb,hnl->hbl", high, low, preferred_element_type=F32)
    closed = jnp.where(marked > 0.5, NEG, 0.0)
    closed = jnp.concatenate(
        (jnp.full((heads, NCTX * NBLK + 1, BLOCK), NEG, F32), closed), axis=1
    )
    hops = slash_offsets // BLOCK
    marks = jnp.stack(
        [
            jnp.stack(
                [
                    lax.dynamic_slice_in_dim(
                        closed[h], ctx * NBLK - hops[h, band] + NCTX * NBLK, NBLK + 1, 0
                    )
                    for band in range(3)
                ]
            )
            for h in range(heads)
        ]
    )
    marks = jnp.concatenate((marks[:, :, :-1], marks[:, :, 1:]), axis=3)

    near = jnp.concatenate((ctx_next(local[:, TOK - BLOCK :]), local), axis=1)
    spots = (vertical_keys - base)[:, None, :]
    state = []
    for distance in (0, 1, 3, 2):
        state = near_attention(
            piece_rows[distance : distance + 1], q_pieces[distance], vert, near, spots, marks, state
        )

    far_hops = hops[:, 1:]
    shifts = (ctx % NBLK + lax.dynamic_index_in_dim(far_hops, ctx // NBLK, 0, False)) // NBLK
    windows = lax.all_to_all(
        spread_windows(shifts, table), "ctx", split_axis=0, concat_axis=0, tiled=True
    ).reshape(heads, NBLK, 2, BLOCK, 2 * DH)
    orders = far_hops % NBLK
    last = jnp.stack(
        [
            jnp.stack(
                [
                    lax.dynamic_index_in_dim(
                        windows[h, :, band], (2 * NBLK - 1 - orders[h, band]) % NBLK, 0, False
                    )
                    for band in range(2)
                ]
            )
            for h in range(heads)
        ]
    )
    halo = ctx_next(last)
    prior, stats, query = state
    return far_attention(orders.reshape(-1), query, prior, stats, windows, halo, marks)


def solution(mesh):
    in_specs = (
        P(("ctx", "tp"), None),
        P(("ctx", "tp"), None),
        P(("ctx", "tp"), None),
        P("tp", None),
        P("tp", None),
    )
    out_specs = P("ctx", "tp")
    return jax.shard_map(shards, mesh=mesh, in_specs=in_specs, out_specs=out_specs, check_vma=False)
```

```python
import functools

import jax
import jax.numpy as jnp
from jax import lax
from jax.experimental import pallas as pl
from jax.experimental.pallas import tpu as pltpu
from jax.sharding import PartitionSpec as P

HQ = 64
KVH = 8
DH = 128
NVERT = 1024
GROUP = HQ // KVH
BLOCK = 64
CAP = 96
SLOTS = 8
NX, NY, NCORE, NTP = 4, 4, 2, 4
NCTX = NX * NY * NCORE
TOK = 1024
NBLK = TOK // BLOCK
KEPT = NVERT // NCTX
PIECE = TOK // NTP
LOG2_SCALE = 1.4426950408889634 * DH**-0.5
NEG = -1e30
BF16 = jnp.bfloat16
F32 = jnp.float32
VMEM_LIMIT = 60 * 2**20


def params():
    return pltpu.CompilerParams(vmem_limit_bytes=VMEM_LIMIT)


def dot_t(left, right):
    return lax.dot_general(left, right, (((1,), (1,)), ((), ())), preferred_element_type=F32)


def tp_shift(block, distance):
    return lax.ppermute(block, "tp", [(i, (i + distance) % NTP) for i in range(NTP)])


def ctx_route(block, move):
    pairs = []
    for x in range(NX):
        for y in range(NY):
            for core in range(NCORE):
                to_x, to_y, to_core = move(x, y, core)
                source = (x * NY + y) * NCORE + core
                target = ((to_x % NX) * NY + to_y % NY) * NCORE + to_core % NCORE
                pairs.append((source, target))
    return lax.ppermute(block, "ctx", pairs)


def ctx_next(block):
    return lax.ppermute(block, "ctx", [(i, i + 1) for i in range(NCTX - 1)])


def join_kernel(rows_ref, keys_ref, p0, p1, p2, p3, local_ref, send_ref):
    for distance, piece in enumerate((p0, p1, p2, p3)):
        first = pl.multiple_of(rows_ref[distance] * PIECE, PIECE)
        local_ref[:, pl.ds(first, PIECE), :] = piece[...]
    spots = lax.broadcasted_iota(jnp.int32, (NCTX * SLOTS, TOK), 1)
    chosen = []
    for head in range(2):
        pick = jnp.where(keys_ref[head] == spots, 1.0, 0.0).astype(BF16)
        rows = jnp.dot(pick, local_ref[head], preferred_element_type=F32)
        chosen.append(rows.reshape(NCTX, SLOTS, 2 * DH))
        for block in range(NBLK):
            send_ref[head * NBLK + block, :BLOCK, :] = local_ref[
                head, block * BLOCK : (block + 1) * BLOCK, :
            ]
    send_ref[:, BLOCK:, :] = jnp.concatenate(chosen, axis=1).astype(BF16)


def join_pieces(rows, keys, pieces):
    vmem = pl.BlockSpec(memory_space=pltpu.VMEM)
    return pl.pallas_call(
        join_kernel,
        in_specs=[pl.BlockSpec(memory_space=pltpu.SMEM)] + [vmem] * 5,
        out_specs=[vmem, vmem],
        out_shape=[
            jax.ShapeDtypeStruct((2, TOK, 2 * DH), BF16),
            jax.ShapeDtypeStruct((NCTX, BLOCK + 2 * SLOTS, 2 * DH), BF16),
        ],
        compiler_params=params(),
    )(rows, keys, *pieces)


def last_kernel(order_ref, *refs):
    for i in range(4):
        refs[4][i // 2, i % 2] = refs[i][0, 0, 0]


def last_blocks(orders, windows):
    def block(i):
        return pl.BlockSpec((1, 1, 1, BLOCK, 2 * DH), lambda g, s: (i // 2, s[i], i % 2, 0, 0))

    return pl.pallas_call(
        last_kernel,
        grid_spec=pltpu.PrefetchScalarGridSpec(
            num_scalar_prefetch=1,
            grid=(1,),
            in_specs=[block(i) for i in range(4)],
            out_specs=pl.BlockSpec((2, 2, BLOCK, 2 * DH), lambda g, s: (0, 0, 0, 0)),
        ),
        out_shape=jax.ShapeDtypeStruct((2, 2, BLOCK, 2 * DH), BF16),
        compiler_params=params(),
    )(orders, windows, windows, windows, windows)


def keep_kernel(first_ref, rows_ref, out_ref, total):
    total[...] = jnp.zeros_like(total)
    slot = lax.broadcasted_iota(jnp.int32, (SLOTS, 2 * DH), 0)
    for source in range(NCTX):
        for head in range(2):
            first = first_ref[head, source]
            rows = rows_ref[source].astype(F32)[head * SLOTS : (head + 1) * SLOTS]
            group = pl.multiple_of(first // SLOTS * SLOTS, SLOTS)
            late = slot >= lax.rem(first, SLOTS)
            total[head, pl.ds(group, SLOTS), :] += jnp.where(late, rows, 0.0)
            total[head, pl.ds(group + SLOTS, SLOTS), :] += jnp.where(late, 0.0, rows)
    out_ref[...] = total[:, :KEPT, :].astype(BF16)


def keep_verticals(firsts, table):
    return pl.pallas_call(
        keep_kernel,
        grid_spec=pltpu.PrefetchScalarGridSpec(
            num_scalar_prefetch=1,
            grid=(1,),
            in_specs=[pl.BlockSpec((NCTX, 2 * SLOTS, 2 * DH), lambda i, s: (0, BLOCK // 16, 0))],
            out_specs=pl.BlockSpec((2, KEPT, 2 * DH), lambda i, s: (0, 0, 0)),
            scratch_shapes=[pltpu.VMEM((2, KEPT + 2 * SLOTS, 2 * DH), F32)],
        ),
        out_shape=jax.ShapeDtypeStruct((2, KEPT, 2 * DH), BF16),
        compiler_params=params(),
    )(firsts, table)


def spread_kernel(shift_ref, table_ref, out_ref):
    group = pl.program_id(0)
    for i in range(8):
        for band in range(2):
            source = jnp.maximum(group * 8 + i - shift_ref[band], 0)
            out_ref[i, band] = table_ref[source, :BLOCK, :]


def spread_windows(shifts, table):
    return pl.pallas_call(
        spread_kernel,
        grid_spec=pltpu.PrefetchScalarGridSpec(
            num_scalar_prefetch=1,
            grid=(NCTX // 8,),
            in_specs=[pl.BlockSpec(table.shape, lambda g, s: (0, 0, 0))],
            out_specs=pl.BlockSpec((8, 2, BLOCK, 2 * DH), lambda g, s: (g, 0, 0, 0)),
        ),
        out_shape=jax.ShapeDtypeStruct((NCTX, 2, BLOCK, 2 * DH), BF16),
        compiler_params=params(),
    )(shifts, table)


def stack_heads(ref, first):
    return jnp.concatenate(
        [ref[first : first + BLOCK, g * DH : (g + 1) * DH] for g in range(GROUP)], axis=0
    )


def band_bias():
    row = lax.broadcasted_iota(jnp.int32, (BLOCK, 2 * BLOCK), 0)
    column = lax.broadcasted_iota(jnp.int32, (BLOCK, 2 * BLOCK), 1)
    distance = row - column + BLOCK
    return jnp.where((distance >= 0) & (distance < BLOCK), 0.0, NEG)


def masked(scores, bias):
    width = scores.shape[1]
    return (scores.reshape(GROUP, BLOCK, width) + bias[None]).reshape(GROUP * BLOCK, width)


def pack_levels(levels):
    lanes = lax.broadcasted_iota(jnp.int32, (BLOCK, DH), 1)
    packed = jnp.zeros((BLOCK, DH), F32)
    for g in range(GROUP):
        packed = jnp.where(lanes == g, levels[g * BLOCK : (g + 1) * BLOCK], packed)
    high = packed.astype(BF16)
    rest = packed - high.astype(F32)
    middle = rest.astype(BF16)
    low = (rest - middle.astype(F32)).astype(BF16)
    terms = high.astype(F32) + pltpu.roll(middle.astype(F32), GROUP, 1)
    return (terms + pltpu.roll(low.astype(F32), 2 * GROUP, 1)).astype(BF16)


def level_picks():
    lane = lax.broadcasted_iota(jnp.int32, (DH, GROUP * DH), 0)
    head = lax.broadcasted_iota(jnp.int32, (DH, GROUP * DH), 1) // DH
    pick = (lane < 3 * GROUP) & (lane % GROUP == head)
    return jnp.where(pick, 1.0, 0.0).astype(BF16)


def spread_levels(packed, picks):
    spread = jnp.dot(packed, picks, preferred_element_type=F32)
    return jnp.concatenate([spread[:, g * DH : (g + 1) * DH] for g in range(GROUP)], axis=0)


def near_kernel(rows_ref, *refs):
    q_refs, vert_refs = refs[:NTP], refs[NTP : NTP + 8]
    near_ref, spot_ref, mark_ref = refs[NTP + 8 : NTP + 11]
    out_ref, stat_ref, copy_ref, vert_ref, band_ref = refs[-5:]
    piece = pl.program_id(0)
    for i in range(NTP):

        @pl.when(piece == i)
        def _():
            copy_ref[0] = q_refs[i][...]

    @pl.when(piece == 0)
    def _():
        for number, part in enumerate(vert_refs):
            for i in range(4):
                first = (number * 4 + i) * KEPT
                vert_ref[first : first + KEPT, : 2 * DH] = part[i, 0]
        vert_ref[:, 2 * DH :] = jnp.ones((NVERT, DH), BF16)
        band_ref[:, : 2 * DH] = near_ref[0]
        band_ref[:, 2 * DH :] = jnp.ones((TOK + BLOCK, DH), BF16)

    bias = band_bias()

    def score(sub):
        block = rows_ref[piece] * (PIECE // BLOCK) + sub
        query = stack_heads(copy_ref.at[0], sub * BLOCK)
        first = pl.multiple_of(block * BLOCK, BLOCK)
        near = jnp.concatenate(
            [band_ref[pl.ds(first, BLOCK), :], band_ref[pl.ds(first + BLOCK, BLOCK), :]], axis=0
        )
        return block, near, dot_t(query, vert_ref[:, :DH]), dot_t(query, near[:, :DH])

    def weigh(block, near, vert_s, near_s):
        position = block * BLOCK + lax.broadcasted_iota(jnp.int32, (BLOCK, NVERT), 0)
        vert_s = masked(vert_s, jnp.where(spot_ref[0] <= position, 0.0, NEG))
        near_s = masked(near_s, bias + mark_ref[0, 0, pl.ds(block, 1), :])
        top = near_s
        for first in range(0, NVERT, DH):
            top = jnp.maximum(top, vert_s[:, first : first + DH])
        top = jnp.max(top, axis=-1, keepdims=True) * LOG2_SCALE
        vert_w = jnp.exp2(vert_s * LOG2_SCALE - top).astype(BF16)
        near_w = jnp.exp2(near_s * LOG2_SCALE - top).astype(BF16)
        return near, top, vert_w, near_w

    def finish(sub, near, top, vert_w, near_w):
        both = jnp.dot(vert_w, vert_ref[:, DH:], preferred_element_type=F32)
        both = both + jnp.dot(
            near_w, near[:, DH:], preferred_element_type=F32
        )
        total = both[:, DH:]
        out = (both[:, :DH] / total).astype(BF16)
        rows = slice(sub * BLOCK, (sub + 1) * BLOCK)
        stat_ref[0, rows, :] = pack_levels(top + jnp.log2(total))
        for g in range(GROUP):
            out_ref[0, rows, g * DH : (g + 1) * DH] = out[g * BLOCK : (g + 1) * BLOCK]

    subtiles = PIECE // BLOCK
    scored, weighed = score(0), None
    for sub in range(subtiles):
        following = score(sub + 1) if sub + 1 < subtiles else None
        current = weigh(*scored)
        if weighed is not None:
            finish(sub - 1, *weighed)
        scored, weighed = following, current
    finish(subtiles - 1, *weighed)


def near_attention(head, rows, queries, vert, near, spots, marks):
    wide = GROUP * DH
    here = lambda p, s: (p, 0, 0)
    return pl.pallas_call(
        near_kernel,
        grid_spec=pltpu.PrefetchScalarGridSpec(
            num_scalar_prefetch=1,
            grid=(NTP,),
            in_specs=[pl.BlockSpec((PIECE, wide), lambda p, s: (0, 0))] * NTP
            + [pl.BlockSpec((4, 1, KEPT, 2 * DH), lambda p, s: (0, head, 0, 0))] * 8
            + [
                pl.BlockSpec((1, TOK + BLOCK, 2 * DH), lambda p, s: (head, 0, 0)),
                pl.BlockSpec((1, 1, NVERT), lambda p, s: (head, 0, 0)),
                pl.BlockSpec((1, 1, NBLK, 2 * BLOCK), lambda p, s: (head, 0, 0, 0)),
            ],
            out_specs=[
                pl.BlockSpec((1, PIECE, wide), here),
                pl.BlockSpec((1, PIECE, DH), here),
                pl.BlockSpec((1, PIECE, wide), here),
            ],
            scratch_shapes=[
                pltpu.VMEM((NVERT, 3 * DH), BF16),
                pltpu.VMEM((TOK + BLOCK, 3 * DH), BF16),
            ],
        ),
        out_shape=[
            jax.ShapeDtypeStruct((NTP, PIECE, wide), BF16),
            jax.ShapeDtypeStruct((NTP, PIECE, DH), BF16),
            jax.ShapeDtypeStruct((NTP, PIECE, wide), BF16),
        ],
        cost_estimate=pl.CostEstimate(flops=10**9, bytes_accessed=2**20, transcendentals=0),
        compiler_params=params(),
    )(rows, *queries, *vert, near, spots, marks)


def far_kernel(
    rows_ref,
    order_ref,
    q_ref,
    prior_ref,
    stat_ref,
    far_ref,
    halo_ref,
    mark_ref,
    done_ref,
    out_ref,
    keys,
    picks,
):
    piece = pl.program_id(0)

    @pl.when(piece == 0)
    def _():
        picks[...] = level_picks()
        for band in range(2):
            keys[band, :BLOCK, :] = halo_ref[0, band]
            for block in range(NBLK):
                source = lax.rem(block + NBLK - order_ref[band], NBLK)
                keys[band, (block + 1) * BLOCK : (block + 2) * BLOCK, :] = far_ref[0, source, band]

    ones = jnp.ones((4 * BLOCK, DH), BF16)
    bias = band_bias()
    for sub in range(PIECE // BLOCK):
        block = rows_ref[piece] * (PIECE // BLOCK) + sub
        first = pl.multiple_of(block * BLOCK, BLOCK)
        rows = slice(sub * BLOCK, (sub + 1) * BLOCK)
        query = stack_heads(q_ref.at[0], sub * BLOCK)
        near = jnp.concatenate([keys[band, pl.ds(first, 2 * BLOCK), :] for band in range(2)], axis=0)
        scores = dot_t(query, near[:, :DH])
        halves = [
            masked(
                scores[:, band * DH : (band + 1) * DH],
                bias + mark_ref[0, 1 + band, pl.ds(block, 1), :],
            )
            for band in range(2)
        ]
        level = spread_levels(stat_ref[0, rows, :], picks[...])
        top = jnp.max(jnp.maximum(halves[0], halves[1]), axis=-1, keepdims=True) * LOG2_SCALE
        top = jnp.maximum(top, level)
        weight = jnp.concatenate(
            [jnp.exp2(half * LOG2_SCALE - top).astype(BF16) for half in halves], axis=1
        )
        both = jnp.dot(
            weight, jnp.concatenate([near[:, DH:], ones], axis=1), preferred_element_type=F32
        )
        prior_w = jnp.exp2(level - top)
        total = both[:, DH:] + prior_w
        prior = stack_heads(prior_ref.at[0], sub * BLOCK).astype(F32)
        out = ((both[:, :DH] + prior * prior_w) / total).astype(BF16)
        for g in range(GROUP):
            out_ref[rows, g * DH : (g + 1) * DH] = out[g * BLOCK : (g + 1) * BLOCK]


def far_attention(head, rows, orders, query, prior, stats, far, halo, marks, done):
    wide = GROUP * DH
    here = lambda p, s, o: (p, 0, 0)
    return pl.pallas_call(
        far_kernel,
        grid_spec=pltpu.PrefetchScalarGridSpec(
            num_scalar_prefetch=2,
            grid=(NTP,),
            in_specs=[
                pl.BlockSpec((1, PIECE, wide), here),
                pl.BlockSpec((1, PIECE, wide), here),
                pl.BlockSpec((1, PIECE, DH), here),
                pl.BlockSpec((1, NBLK, 2, BLOCK, 2 * DH), lambda p, s, o: (head, 0, 0, 0, 0)),
                pl.BlockSpec((1, 2, BLOCK, 2 * DH), lambda p, s, o: (head, 0, 0, 0)),
                pl.BlockSpec((1, 3, NBLK, 2 * BLOCK), lambda p, s, o: (head, 0, 0, 0)),
                pl.BlockSpec(memory_space=pl.ANY),
            ],
            out_specs=pl.BlockSpec((PIECE, wide), lambda p, s, o: (s[p], head)),
            scratch_shapes=[
                pltpu.VMEM((2, TOK + BLOCK, 2 * DH), BF16),
                pltpu.VMEM((DH, GROUP * DH), BF16),
            ],
        ),
        out_shape=jax.ShapeDtypeStruct((TOK, 2 * wide), BF16),
        input_output_aliases={8: 0},
        compiler_params=params(),
    )(rows, orders, query, prior, stats, far, halo, marks, done)


def attend_kernel(rows_ref, order_ref, *refs):
    q_refs, vert_refs = refs[:NTP], refs[NTP : NTP + 8]
    near_ref, far_ref, halo_ref, spot_ref, mark_ref = refs[NTP + 8 : NTP + 13]
    out_ref, query_ref, vert_ref, band_ref = refs[-4:]
    piece = pl.program_id(0)
    for i in range(NTP):

        @pl.when(piece == i)
        def _():
            query_ref[...] = q_refs[i][...]

    @pl.when(piece == 0)
    def _():
        for number, part in enumerate(vert_refs):
            for i in range(4):
                first = (number * 4 + i) * KEPT
                vert_ref[first : first + KEPT, : 2 * DH] = part[i, 0]
        vert_ref[:, 2 * DH :] = jnp.ones((NVERT, DH), BF16)
        for band in range(2):
            band_ref[band, :BLOCK, :] = halo_ref[0, band]
            for block in range(NBLK):
                source = lax.rem(block + NBLK - order_ref[band], NBLK)
                band_ref[band, (block + 1) * BLOCK : (block + 2) * BLOCK, :] = far_ref[
                    0, source, band
                ]

    ones = jnp.ones((6 * BLOCK, DH), BF16)
    bias = band_bias()

    def score(sub):
        block = rows_ref[piece] * (PIECE // BLOCK) + sub
        query = stack_heads(query_ref, sub * BLOCK)
        window = pl.ds(pl.multiple_of(block * BLOCK, BLOCK), 2 * BLOCK)
        band = jnp.concatenate(
            [near_ref[0, window, :], band_ref[0, window, :], band_ref[1, window, :]], axis=0
        )
        return block, band, dot_t(query, vert_ref[:, :DH]), dot_t(query, band[:, :DH])

    def weigh(block, band, vert_s, band_s):
        position = block * BLOCK + lax.broadcasted_iota(jnp.int32, (BLOCK, NVERT), 0)
        vert_s = masked(vert_s, jnp.where(spot_ref[0] <= position, 0.0, NEG))
        band_bias_s = jnp.concatenate(
            [bias + mark_ref[0, i, pl.ds(block, 1), :] for i in range(3)], axis=1
        )
        band_s = masked(band_s, band_bias_s)
        top = band_s[:, :DH]
        for first in range(DH, 3 * DH, DH):
            top = jnp.maximum(top, band_s[:, first : first + DH])
        for first in range(0, NVERT, DH):
            top = jnp.maximum(top, vert_s[:, first : first + DH])
        top = jnp.max(top, axis=-1, keepdims=True) * LOG2_SCALE
        vert_w = jnp.exp2(vert_s * LOG2_SCALE - top).astype(BF16)
        band_w = jnp.exp2(band_s * LOG2_SCALE - top).astype(BF16)
        return band, vert_w, band_w

    def finish(sub, band, vert_w, band_w):
        both = jnp.dot(vert_w, vert_ref[:, DH:], preferred_element_type=F32)
        both = both + jnp.dot(
            band_w, jnp.concatenate([band[:, DH:], ones], axis=1), preferred_element_type=F32
        )
        out = (both[:, :DH] / both[:, DH:]).astype(BF16)
        rows = slice(sub * BLOCK, (sub + 1) * BLOCK)
        for g in range(GROUP):
            out_ref[rows, g * DH : (g + 1) * DH] = out[g * BLOCK : (g + 1) * BLOCK]

    subtiles = PIECE // BLOCK
    scored, weighed = score(0), None
    for sub in range(subtiles):
        following = score(sub + 1) if sub + 1 < subtiles else None
        current = weigh(*scored)
        if weighed is not None:
            finish(sub - 1, *weighed)
        scored, weighed = following, current
    finish(subtiles - 1, *weighed)


def attend(head, rows, orders, queries, vert, near, far, halo, spots, marks):
    wide = GROUP * DH
    scored = TOK * GROUP * (NVERT + 6 * BLOCK)
    return pl.pallas_call(
        attend_kernel,
        grid_spec=pltpu.PrefetchScalarGridSpec(
            num_scalar_prefetch=2,
            grid=(NTP,),
            in_specs=[pl.BlockSpec((PIECE, wide), lambda p, s, o: (0, 0))] * NTP
            + [pl.BlockSpec((4, 1, KEPT, 2 * DH), lambda p, s, o: (0, head, 0, 0))] * 8
            + [
                pl.BlockSpec((1, TOK + BLOCK, 2 * DH), lambda p, s, o: (head, 0, 0)),
                pl.BlockSpec((1, NBLK, 2, BLOCK, 2 * DH), lambda p, s, o: (head, 0, 0, 0, 0)),
                pl.BlockSpec((1, 2, BLOCK, 2 * DH), lambda p, s, o: (head, 0, 0, 0)),
                pl.BlockSpec((1, 1, NVERT), lambda p, s, o: (head, 0, 0)),
                pl.BlockSpec((1, 3, NBLK, 2 * BLOCK), lambda p, s, o: (head, 0, 0, 0)),
            ],
            out_specs=pl.BlockSpec((PIECE, wide), lambda p, s, o: (s[p], head)),
            scratch_shapes=[
                pltpu.VMEM((PIECE, wide), BF16),
                pltpu.VMEM((NVERT, 3 * DH), BF16),
                pltpu.VMEM((2, TOK + BLOCK, 2 * DH), BF16),
            ],
        ),
        out_shape=jax.ShapeDtypeStruct((TOK, 2 * wide), BF16),
        cost_estimate=pl.CostEstimate(
            flops=scored * 4 * 2 * DH, bytes_accessed=6 * 2**20, transcendentals=scored
        ),
        compiler_params=params(),
    )(rows, orders, *queries, *vert, near, far, halo, spots, marks)


def shards(queries, key_rows, value_rows, vertical_keys, slash_offsets):
    tp = lax.axis_index("tp")
    ctx = lax.axis_index("ctx")
    base = ctx * TOK
    heads = vertical_keys.shape[0]
    hops = slash_offsets // BLOCK
    far_hops = hops[:, 1:]

    kv = jnp.concatenate(
        (key_rows.reshape(PIECE, KVH, DH), value_rows.reshape(PIECE, KVH, DH)), axis=2
    ).transpose(1, 0, 2)
    kv_pieces = []
    for distance in range(NTP):
        part = lax.dynamic_slice_in_dim(kv, heads * ((tp + distance) % NTP), heads, 0)
        kv_pieces.append(tp_shift(part, distance) if distance else part)

    ranked = vertical_keys.reshape(heads, KEPT // SLOTS, SLOTS, NCTX) - base
    own_keys = jnp.max(jnp.where((ranked >= 0) & (ranked < TOK), ranked, -1), axis=1)
    own_keys = own_keys.transpose(0, 2, 1).reshape(heads, NCTX * SLOTS, 1)
    devices = jnp.arange(NCTX, dtype=jnp.int32)
    started = jnp.sum(
        vertical_keys[:, None, :] < (devices * TOK)[None, :, None], axis=2, dtype=jnp.int32
    )
    kept_first = (started - ctx + NCTX - 1) // NCTX
    piece_rows = (tp + NTP - jnp.arange(NTP, dtype=jnp.int32)) % NTP

    x, y, core = ctx // 8, (ctx // 2) % 4, ctx % 2
    kept_spots = (vertical_keys - base).reshape(heads, KEPT, NX, NY, NCORE)
    for axis, place, size in ((2, x, NX), (3, y, NY), (4, core, NCORE)):
        turned = jnp.flip(kept_spots, axis)
        turned = jnp.concatenate((turned, turned), axis=axis)
        kept_spots = lax.dynamic_slice_in_dim(turned, size - 1 - place, size, axis)
    spots = kept_spots.transpose(0, 4, 2, 3, 1).reshape(heads, 1, NVERT)

    blocks = jnp.arange(-1, NBLK, dtype=jnp.int32) + ctx * NBLK - hops[:, :, None]
    blocks = blocks.reshape(heads, 3 * (NBLK + 1))
    high = (vertical_keys[:, :, None] // BLOCK == blocks[:, None, :]).astype(BF16)
    low = (vertical_keys[:, :, None] % BLOCK == jnp.arange(BLOCK)).astype(BF16)
    marked = jnp.einsum("hnb,hnl->hbl", high, low, preferred_element_type=F32)
    marks = jnp.where((marked > 0.5) | (blocks < 0)[:, :, None], NEG, 0.0)
    marks = marks.reshape(heads, 3, NBLK + 1, BLOCK)
    marks = jnp.concatenate((marks[:, :, :-1], marks[:, :, 1:]), axis=3)

    def query_parts(head):
        wide = GROUP * DH
        firsts = [wide * (heads * ((tp + step) % NTP) + head) for step in range(NTP)]
        return [lax.dynamic_slice_in_dim(queries, first, wide, 1) for first in firsts]

    def send_queries(parts):
        return parts[:1] + [tp_shift(parts[step], step) for step in (1, 2, 3)]

    first_parts, second_parts = query_parts(0), query_parts(1)
    received, first_parts, own_keys = lax.optimization_barrier(
        (kv_pieces[1:], first_parts, own_keys)
    )
    first_queries = send_queries(first_parts)
    local, sent = join_pieces(piece_rows, own_keys, kv_pieces[:1] + received)
    beside = ctx_next(local[:, TOK - BLOCK :])

    table = lax.all_to_all(sent, "ctx", split_axis=0, concat_axis=0, tiled=True)
    orders = far_hops % NBLK
    table, marks, spots, kept_first, orders = lax.optimization_barrier(
        (table, marks, spots, kept_first, orders)
    )

    kept = keep_verticals(kept_first, table)
    along_y = [kept] + [
        ctx_route(kept, lambda x, y, core, step=step: (x, y + step, core)) for step in (1, 2, 3)
    ]
    along_y, beside, first_queries, second_parts = lax.optimization_barrier(
        (along_y, beside, first_queries, second_parts)
    )
    second_queries = send_queries(second_parts)
    along_y = jnp.stack(along_y)
    along_x = [along_y] + [
        ctx_route(along_y, lambda x, y, core, step=step: (x + step, y, core)) for step in (1, 2, 3)
    ]
    across = [ctx_route(part, lambda x, y, core: (x, y, core + 1)) for part in along_x]
    shifts = (ctx % NBLK + jnp.where(ctx < NBLK, far_hops[0], far_hops[1])) // NBLK
    spread = spread_windows(shifts, table)
    near = jnp.concatenate((beside, local), axis=1)
    spread, across, near = lax.optimization_barrier((spread, across, near))
    vert = along_x + across

    windows = lax.all_to_all(
        spread, "ctx", split_axis=0, concat_axis=0, tiled=True
    ).reshape(heads, NBLK, 2, BLOCK, 2 * DH)
    prior = near_attention(0, piece_rows, first_queries, vert, near, spots, marks)
    windows, prior = lax.optimization_barrier((windows, prior))
    last = last_blocks((2 * NBLK - 1 - orders).reshape(-1) % NBLK, windows)
    halo = ctx_next(last)
    out = attend(
        1, piece_rows, orders[1], second_queries, vert, near, windows, halo, spots, marks
    )
    prior, stats, query = prior
    return far_attention(
        0, piece_rows, orders[0], query, prior, stats, windows, halo, marks, out
    )


def solution(mesh):
    in_specs = (
        P(("ctx", "tp"), None),
        P(("ctx", "tp"), None),
        P(("ctx", "tp"), None),
        P("tp", None),
        P("tp", None),
    )
    out_specs = P("ctx", "tp")
    return jax.shard_map(shards, mesh=mesh, in_specs=in_specs, out_specs=out_specs, check_vma=False)
```

```python
import functools

import jax
import jax.numpy as jnp
from jax import lax
from jax.experimental import pallas as pl
from jax.experimental.pallas import tpu as pltpu
from jax.sharding import PartitionSpec as P

HQ = 64
KVH = 8
DH = 128
NVERT = 1024
GROUP = HQ // KVH
BLOCK = 64
CAP = 96
SLOTS = 8
NX, NY, NCORE, NTP = 4, 4, 2, 4
NCTX = NX * NY * NCORE
TOK = 1024
NBLK = TOK // BLOCK
KEPT = NVERT // NCTX
PIECE = TOK // NTP
LOG2_SCALE = 1.4426950408889634 * DH**-0.5
NEG = -1e30
BF16 = jnp.bfloat16
F32 = jnp.float32
VMEM_LIMIT = 63 * 2**20 + 2**19


def params():
    return pltpu.CompilerParams(vmem_limit_bytes=VMEM_LIMIT)


def dot_t(left, right):
    return lax.dot_general(left, right, (((1,), (1,)), ((), ())), preferred_element_type=F32)


def tp_shift(block, distance):
    return lax.ppermute(block, "tp", [(i, (i + distance) % NTP) for i in range(NTP)])


def ctx_route(block, move):
    pairs = []
    for x in range(NX):
        for y in range(NY):
            for core in range(NCORE):
                to_x, to_y, to_core = move(x, y, core)
                source = (x * NY + y) * NCORE + core
                target = ((to_x % NX) * NY + to_y % NY) * NCORE + to_core % NCORE
                pairs.append((source, target))
    return lax.ppermute(block, "ctx", pairs)


def ctx_next(block):
    return lax.ppermute(block, "ctx", [(i, i + 1) for i in range(NCTX - 1)])


def join_kernel(rows_ref, keys_ref, p0, p1, p2, p3, local_ref, send_ref):
    for distance, piece in enumerate((p0, p1, p2, p3)):
        first = pl.multiple_of(rows_ref[distance] * PIECE, PIECE)
        local_ref[:, pl.ds(first, PIECE), :] = piece[...]
    spots = lax.broadcasted_iota(jnp.int32, (NCTX * SLOTS, TOK), 1)
    chosen = []
    for head in range(2):
        pick = jnp.where(keys_ref[head] == spots, 1.0, 0.0).astype(BF16)
        rows = jnp.dot(pick, local_ref[head], preferred_element_type=F32)
        chosen.append(rows.reshape(NCTX, SLOTS, 2 * DH))
        for block in range(NBLK):
            send_ref[head * NBLK + block, :BLOCK, :] = local_ref[
                head, block * BLOCK : (block + 1) * BLOCK, :
            ]
    send_ref[:, BLOCK:, :] = jnp.concatenate(chosen, axis=1).astype(BF16)


def join_pieces(rows, keys, pieces):
    vmem = pl.BlockSpec(memory_space=pltpu.VMEM)
    return pl.pallas_call(
        join_kernel,
        in_specs=[pl.BlockSpec(memory_space=pltpu.SMEM)] + [vmem] * 5,
        out_specs=[vmem, vmem],
        out_shape=[
            jax.ShapeDtypeStruct((2, TOK, 2 * DH), BF16),
            jax.ShapeDtypeStruct((NCTX, BLOCK + 2 * SLOTS, 2 * DH), BF16),
        ],
        compiler_params=params(),
    )(rows, keys, *pieces)


def last_kernel(order_ref, *refs):
    for i in range(4):
        refs[4][i // 2, i % 2] = refs[i][0, 0, 0]


def last_blocks(orders, windows):
    def block(i):
        return pl.BlockSpec((1, 1, 1, BLOCK, 2 * DH), lambda g, s: (i // 2, s[i], i % 2, 0, 0))

    return pl.pallas_call(
        last_kernel,
        grid_spec=pltpu.PrefetchScalarGridSpec(
            num_scalar_prefetch=1,
            grid=(1,),
            in_specs=[block(i) for i in range(4)],
            out_specs=pl.BlockSpec((2, 2, BLOCK, 2 * DH), lambda g, s: (0, 0, 0, 0)),
        ),
        out_shape=jax.ShapeDtypeStruct((2, 2, BLOCK, 2 * DH), BF16),
        compiler_params=params(),
    )(orders, windows, windows, windows, windows)


def keep_kernel(first_ref, rows_ref, out_ref, total):
    total[...] = jnp.zeros_like(total)
    slot = lax.broadcasted_iota(jnp.int32, (SLOTS, 2 * DH), 0)
    for source in range(NCTX):
        for head in range(2):
            first = first_ref[head, source]
            rows = rows_ref[source].astype(F32)[head * SLOTS : (head + 1) * SLOTS]
            group = pl.multiple_of(first // SLOTS * SLOTS, SLOTS)
            late = slot >= lax.rem(first, SLOTS)
            total[head, pl.ds(group, SLOTS), :] += jnp.where(late, rows, 0.0)
            total[head, pl.ds(group + SLOTS, SLOTS), :] += jnp.where(late, 0.0, rows)
    out_ref[...] = total[:, :KEPT, :].astype(BF16)


def keep_verticals(firsts, table):
    return pl.pallas_call(
        keep_kernel,
        grid_spec=pltpu.PrefetchScalarGridSpec(
            num_scalar_prefetch=1,
            grid=(1,),
            in_specs=[pl.BlockSpec((NCTX, 2 * SLOTS, 2 * DH), lambda i, s: (0, BLOCK // 16, 0))],
            out_specs=pl.BlockSpec((2, KEPT, 2 * DH), lambda i, s: (0, 0, 0)),
            scratch_shapes=[pltpu.VMEM((2, KEPT + 2 * SLOTS, 2 * DH), F32)],
        ),
        out_shape=jax.ShapeDtypeStruct((2, KEPT, 2 * DH), BF16),
        compiler_params=params(),
    )(firsts, table)


def spread_kernel(shift_ref, table_ref, out_ref):
    group = pl.program_id(0)
    for i in range(8):
        for band in range(2):
            source = jnp.maximum(group * 8 + i - shift_ref[band], 0)
            out_ref[i, band] = table_ref[source, :BLOCK, :]


def spread_windows(shifts, table):
    return pl.pallas_call(
        spread_kernel,
        grid_spec=pltpu.PrefetchScalarGridSpec(
            num_scalar_prefetch=1,
            grid=(NCTX // 8,),
            in_specs=[pl.BlockSpec(table.shape, lambda g, s: (0, 0, 0))],
            out_specs=pl.BlockSpec((8, 2, BLOCK, 2 * DH), lambda g, s: (g, 0, 0, 0)),
        ),
        out_shape=jax.ShapeDtypeStruct((NCTX, 2, BLOCK, 2 * DH), BF16),
        compiler_params=params(),
    )(shifts, table)


def stack_heads(ref, first):
    return jnp.concatenate(
        [ref[first : first + BLOCK, g * DH : (g + 1) * DH] for g in range(GROUP)], axis=0
    )


def band_bias():
    row = lax.broadcasted_iota(jnp.int32, (BLOCK, 2 * BLOCK), 0)
    column = lax.broadcasted_iota(jnp.int32, (BLOCK, 2 * BLOCK), 1)
    distance = row - column + BLOCK
    return jnp.where((distance >= 0) & (distance < BLOCK), 0.0, NEG)


def masked(scores, bias):
    width = scores.shape[1]
    return (scores.reshape(GROUP, BLOCK, width) + bias[None]).reshape(GROUP * BLOCK, width)


def pack_levels(levels):
    lanes = lax.broadcasted_iota(jnp.int32, (BLOCK, DH), 1)
    packed = jnp.zeros((BLOCK, DH), F32)
    for g in range(GROUP):
        packed = jnp.where(lanes == g, levels[g * BLOCK : (g + 1) * BLOCK], packed)
    high = packed.astype(BF16)
    rest = packed - high.astype(F32)
    middle = rest.astype(BF16)
    low = (rest - middle.astype(F32)).astype(BF16)
    terms = high.astype(F32) + pltpu.roll(middle.astype(F32), GROUP, 1)
    return (terms + pltpu.roll(low.astype(F32), 2 * GROUP, 1)).astype(BF16)


def level_picks():
    lane = lax.broadcasted_iota(jnp.int32, (DH, GROUP * DH), 0)
    head = lax.broadcasted_iota(jnp.int32, (DH, GROUP * DH), 1) // DH
    pick = (lane < 3 * GROUP) & (lane % GROUP == head)
    return jnp.where(pick, 1.0, 0.0).astype(BF16)


def spread_levels(packed, picks):
    spread = jnp.dot(packed, picks, preferred_element_type=F32)
    return jnp.concatenate([spread[:, g * DH : (g + 1) * DH] for g in range(GROUP)], axis=0)


def near_kernel(rows_ref, *refs):
    q_refs, vert_refs = refs[:NTP], refs[NTP : NTP + 8]
    beside_ref, local_ref, spot_ref, mark_ref = refs[NTP + 8 : NTP + 12]
    out_ref, stat_ref, copy_ref, vert_ref, band_ref = refs[-5:]
    piece = pl.program_id(0)
    for i in range(NTP):

        @pl.when(piece == i)
        def _():
            copy_ref[0] = q_refs[i][...]

    @pl.when(piece == 0)
    def _():
        for number, part in enumerate(vert_refs):
            for i in range(4):
                first = (number * 4 + i) * KEPT
                vert_ref[first : first + KEPT, : 2 * DH] = part[i, 0]
        vert_ref[:, 2 * DH :] = jnp.ones((NVERT, DH), BF16)
        band_ref[:BLOCK, : 2 * DH] = beside_ref[0]
        band_ref[BLOCK:, : 2 * DH] = local_ref[0]
        band_ref[:, 2 * DH :] = jnp.ones((TOK + BLOCK, DH), BF16)

    bias = band_bias()

    def score(sub):
        block = rows_ref[piece] * (PIECE // BLOCK) + sub
        query = stack_heads(copy_ref.at[0], sub * BLOCK)
        first = pl.multiple_of(block * BLOCK, BLOCK)
        near = jnp.concatenate(
            [band_ref[pl.ds(first, BLOCK), :], band_ref[pl.ds(first + BLOCK, BLOCK), :]], axis=0
        )
        return block, near, dot_t(query, vert_ref[:, :DH]), dot_t(query, near[:, :DH])

    def weigh(block, near, vert_s, near_s):
        position = block * BLOCK + lax.broadcasted_iota(jnp.int32, (BLOCK, NVERT), 0)
        vert_s = masked(vert_s, jnp.where(spot_ref[0] <= position, 0.0, NEG))
        near_s = masked(near_s, bias + mark_ref[0, 0, pl.ds(block, 1), :])
        top = near_s
        for first in range(0, NVERT, DH):
            top = jnp.maximum(top, vert_s[:, first : first + DH])
        top = jnp.max(top, axis=-1, keepdims=True) * LOG2_SCALE
        vert_w = jnp.exp2(vert_s * LOG2_SCALE - top).astype(BF16)
        near_w = jnp.exp2(near_s * LOG2_SCALE - top).astype(BF16)
        return near, top, vert_w, near_w

    def finish(sub, near, top, vert_w, near_w):
        both = jnp.dot(vert_w, vert_ref[:, DH:], preferred_element_type=F32)
        both = both + jnp.dot(
            near_w, near[:, DH:], preferred_element_type=F32
        )
        total = both[:, DH:]
        out = (both[:, :DH] / total).astype(BF16)
        rows = slice(sub * BLOCK, (sub + 1) * BLOCK)
        stat_ref[0, rows, :] = pack_levels(top + jnp.log2(total))
        for g in range(GROUP):
            out_ref[0, rows, g * DH : (g + 1) * DH] = out[g * BLOCK : (g + 1) * BLOCK]

    subtiles = PIECE // BLOCK
    scored, weighed = score(0), None
    for sub in range(subtiles):
        following = score(sub + 1) if sub + 1 < subtiles else None
        current = weigh(*scored)
        if weighed is not None:
            finish(sub - 1, *weighed)
        scored, weighed = following, current
    finish(subtiles - 1, *weighed)


def near_attention(head, rows, queries, vert, beside, local, spots, marks):
    wide = GROUP * DH
    here = lambda p, s: (p, 0, 0)
    return pl.pallas_call(
        near_kernel,
        grid_spec=pltpu.PrefetchScalarGridSpec(
            num_scalar_prefetch=1,
            grid=(NTP,),
            in_specs=[pl.BlockSpec((PIECE, wide), lambda p, s: (0, 0))] * NTP
            + [pl.BlockSpec((4, 1, KEPT, 2 * DH), lambda p, s: (0, head, 0, 0))] * 8
            + [
                pl.BlockSpec((1, BLOCK, 2 * DH), lambda p, s: (head, 0, 0)),
                pl.BlockSpec((1, TOK, 2 * DH), lambda p, s: (head, 0, 0)),
                pl.BlockSpec((1, 1, NVERT), lambda p, s: (head, 0, 0)),
                pl.BlockSpec((1, 1, NBLK, 2 * BLOCK), lambda p, s: (head, 0, 0, 0)),
            ],
            out_specs=[
                pl.BlockSpec((1, PIECE, wide), here),
                pl.BlockSpec((1, PIECE, DH), here),
                pl.BlockSpec((1, PIECE, wide), here),
            ],
            scratch_shapes=[
                pltpu.VMEM((NVERT, 3 * DH), BF16),
                pltpu.VMEM((TOK + BLOCK, 3 * DH), BF16),
            ],
        ),
        out_shape=[
            jax.ShapeDtypeStruct((NTP, PIECE, wide), BF16),
            jax.ShapeDtypeStruct((NTP, PIECE, DH), BF16),
            jax.ShapeDtypeStruct((NTP, PIECE, wide), BF16),
        ],
        cost_estimate=pl.CostEstimate(flops=10**9, bytes_accessed=2**20, transcendentals=0),
        compiler_params=params(),
    )(rows, *queries, *vert, beside, local, spots, marks)


def far_kernel(
    rows_ref,
    order_ref,
    q_ref,
    prior_ref,
    stat_ref,
    far_ref,
    halo_ref,
    mark_ref,
    done_ref,
    out_ref,
    keys,
    picks,
):
    piece = pl.program_id(0)

    @pl.when(piece == 0)
    def _():
        picks[...] = level_picks()
        for band in range(2):
            keys[band, :BLOCK, :] = halo_ref[0, band]
            for block in range(NBLK):
                source = lax.rem(block + NBLK - order_ref[band], NBLK)
                keys[band, (block + 1) * BLOCK : (block + 2) * BLOCK, :] = far_ref[0, source, band]

    ones = jnp.ones((4 * BLOCK, DH), BF16)
    bias = band_bias()
    for sub in range(PIECE // BLOCK):
        block = rows_ref[piece] * (PIECE // BLOCK) + sub
        first = pl.multiple_of(block * BLOCK, BLOCK)
        rows = slice(sub * BLOCK, (sub + 1) * BLOCK)
        query = stack_heads(q_ref.at[0], sub * BLOCK)
        near = jnp.concatenate([keys[band, pl.ds(first, 2 * BLOCK), :] for band in range(2)], axis=0)
        scores = dot_t(query, near[:, :DH])
        halves = [
            masked(
                scores[:, band * DH : (band + 1) * DH],
                bias + mark_ref[0, 1 + band, pl.ds(block, 1), :],
            )
            for band in range(2)
        ]
        level = spread_levels(stat_ref[0, rows, :], picks[...])
        top = jnp.max(jnp.maximum(halves[0], halves[1]), axis=-1, keepdims=True) * LOG2_SCALE
        top = jnp.maximum(top, level)
        weight = jnp.concatenate(
            [jnp.exp2(half * LOG2_SCALE - top).astype(BF16) for half in halves], axis=1
        )
        both = jnp.dot(
            weight, jnp.concatenate([near[:, DH:], ones], axis=1), preferred_element_type=F32
        )
        prior_w = jnp.exp2(level - top)
        total = both[:, DH:] + prior_w
        prior = stack_heads(prior_ref.at[0], sub * BLOCK).astype(F32)
        out = ((both[:, :DH] + prior * prior_w) / total).astype(BF16)
        for g in range(GROUP):
            out_ref[rows, g * DH : (g + 1) * DH] = out[g * BLOCK : (g + 1) * BLOCK]


def far_attention(head, rows, orders, query, prior, stats, far, halo, marks, done):
    wide = GROUP * DH
    here = lambda p, s, o: (p, 0, 0)
    return pl.pallas_call(
        far_kernel,
        grid_spec=pltpu.PrefetchScalarGridSpec(
            num_scalar_prefetch=2,
            grid=(NTP,),
            in_specs=[
                pl.BlockSpec((1, PIECE, wide), here),
                pl.BlockSpec((1, PIECE, wide), here),
                pl.BlockSpec((1, PIECE, DH), here),
                pl.BlockSpec((1, NBLK, 2, BLOCK, 2 * DH), lambda p, s, o: (head, 0, 0, 0, 0)),
                pl.BlockSpec((1, 2, BLOCK, 2 * DH), lambda p, s, o: (head, 0, 0, 0)),
                pl.BlockSpec((1, 3, NBLK, 2 * BLOCK), lambda p, s, o: (head, 0, 0, 0)),
                pl.BlockSpec(memory_space=pl.ANY),
            ],
            out_specs=pl.BlockSpec((PIECE, wide), lambda p, s, o: (s[p], head)),
            scratch_shapes=[
                pltpu.VMEM((2, TOK + BLOCK, 2 * DH), BF16),
                pltpu.VMEM((DH, GROUP * DH), BF16),
            ],
        ),
        out_shape=jax.ShapeDtypeStruct((TOK, 2 * wide), BF16),
        input_output_aliases={8: 0},
        compiler_params=params(),
    )(rows, orders, query, prior, stats, far, halo, marks, done)


def attend_kernel(rows_ref, order_ref, *refs):
    q_refs, vert_refs = refs[:NTP], refs[NTP : NTP + 8]
    beside_ref, local_ref, far_ref, halo_ref, spot_ref, mark_ref = refs[NTP + 8 : NTP + 14]
    out_ref, query_ref, vert_ref, band_ref = refs[-4:]
    piece = pl.program_id(0)
    for i in range(NTP):

        @pl.when(piece == i)
        def _():
            query_ref[...] = q_refs[i][...]

    @pl.when(piece == 0)
    def _():
        for number, part in enumerate(vert_refs):
            for i in range(4):
                first = (number * 4 + i) * KEPT
                vert_ref[first : first + KEPT, : 2 * DH] = part[i, 0]
        vert_ref[:, 2 * DH :] = jnp.ones((NVERT, DH), BF16)
        band_ref[2, :BLOCK, :] = beside_ref[0]
        band_ref[2, BLOCK:, :] = local_ref[0]
        for band in range(2):
            band_ref[band, :BLOCK, :] = halo_ref[0, band]
            for block in range(NBLK):
                source = lax.rem(block + NBLK - order_ref[band], NBLK)
                band_ref[band, (block + 1) * BLOCK : (block + 2) * BLOCK, :] = far_ref[
                    0, source, band
                ]

    ones = jnp.ones((6 * BLOCK, DH), BF16)
    bias = band_bias()

    def score(sub):
        block = rows_ref[piece] * (PIECE // BLOCK) + sub
        query = stack_heads(query_ref, sub * BLOCK)
        window = pl.ds(pl.multiple_of(block * BLOCK, BLOCK), 2 * BLOCK)
        band = jnp.concatenate(
            [band_ref[2, window, :], band_ref[0, window, :], band_ref[1, window, :]], axis=0
        )
        return block, band, dot_t(query, vert_ref[:, :DH]), dot_t(query, band[:, :DH])

    def weigh(block, band, vert_s, band_s):
        position = block * BLOCK + lax.broadcasted_iota(jnp.int32, (BLOCK, NVERT), 0)
        vert_s = masked(vert_s, jnp.where(spot_ref[0] <= position, 0.0, NEG))
        band_bias_s = jnp.concatenate(
            [bias + mark_ref[0, i, pl.ds(block, 1), :] for i in range(3)], axis=1
        )
        band_s = masked(band_s, band_bias_s)
        top = band_s[:, :DH]
        for first in range(DH, 3 * DH, DH):
            top = jnp.maximum(top, band_s[:, first : first + DH])
        for first in range(0, NVERT, DH):
            top = jnp.maximum(top, vert_s[:, first : first + DH])
        top = jnp.max(top, axis=-1, keepdims=True) * LOG2_SCALE
        vert_w = jnp.exp2(vert_s * LOG2_SCALE - top).astype(BF16)
        band_w = jnp.exp2(band_s * LOG2_SCALE - top).astype(BF16)
        return band, vert_w, band_w

    def finish(sub, band, vert_w, band_w):
        both = jnp.dot(vert_w, vert_ref[:, DH:], preferred_element_type=F32)
        both = both + jnp.dot(
            band_w, jnp.concatenate([band[:, DH:], ones], axis=1), preferred_element_type=F32
        )
        out = (both[:, :DH] / both[:, DH:]).astype(BF16)
        rows = slice(sub * BLOCK, (sub + 1) * BLOCK)
        for g in range(GROUP):
            out_ref[rows, g * DH : (g + 1) * DH] = out[g * BLOCK : (g + 1) * BLOCK]

    subtiles = PIECE // BLOCK
    scored, weighed = score(0), None
    for sub in range(subtiles):
        following = score(sub + 1) if sub + 1 < subtiles else None
        current = weigh(*scored)
        if weighed is not None:
            finish(sub - 1, *weighed)
        scored, weighed = following, current
    finish(subtiles - 1, *weighed)


def attend(head, rows, orders, queries, vert, beside, local, far, halo, spots, marks):
    wide = GROUP * DH
    scored = TOK * GROUP * (NVERT + 6 * BLOCK)
    return pl.pallas_call(
        attend_kernel,
        grid_spec=pltpu.PrefetchScalarGridSpec(
            num_scalar_prefetch=2,
            grid=(NTP,),
            in_specs=[pl.BlockSpec((PIECE, wide), lambda p, s, o: (0, 0))] * NTP
            + [pl.BlockSpec((4, 1, KEPT, 2 * DH), lambda p, s, o: (0, head, 0, 0))] * 8
            + [
                pl.BlockSpec((1, BLOCK, 2 * DH), lambda p, s, o: (head, 0, 0)),
                pl.BlockSpec((1, TOK, 2 * DH), lambda p, s, o: (head, 0, 0)),
                pl.BlockSpec((1, NBLK, 2, BLOCK, 2 * DH), lambda p, s, o: (head, 0, 0, 0, 0)),
                pl.BlockSpec((1, 2, BLOCK, 2 * DH), lambda p, s, o: (head, 0, 0, 0)),
                pl.BlockSpec((1, 1, NVERT), lambda p, s, o: (head, 0, 0)),
                pl.BlockSpec((1, 3, NBLK, 2 * BLOCK), lambda p, s, o: (head, 0, 0, 0)),
            ],
            out_specs=pl.BlockSpec((PIECE, wide), lambda p, s, o: (s[p], head)),
            scratch_shapes=[
                pltpu.VMEM((PIECE, wide), BF16),
                pltpu.VMEM((NVERT, 3 * DH), BF16),
                pltpu.VMEM((3, TOK + BLOCK, 2 * DH), BF16),
            ],
        ),
        out_shape=jax.ShapeDtypeStruct((TOK, 2 * wide), BF16),
        cost_estimate=pl.CostEstimate(
            flops=scored * 4 * 2 * DH, bytes_accessed=6 * 2**20, transcendentals=scored
        ),
        compiler_params=params(),
    )(rows, orders, *queries, *vert, beside, local, far, halo, spots, marks)


def shards(queries, key_rows, value_rows, vertical_keys, slash_offsets):
    tp = lax.axis_index("tp")
    ctx = lax.axis_index("ctx")
    base = ctx * TOK
    heads = vertical_keys.shape[0]
    hops = slash_offsets // BLOCK
    far_hops = hops[:, 1:]

    kv = jnp.concatenate(
        (key_rows.reshape(PIECE, KVH, DH), value_rows.reshape(PIECE, KVH, DH)), axis=2
    ).transpose(1, 0, 2)
    kv_pieces = []
    for distance in range(NTP):
        part = lax.dynamic_slice_in_dim(kv, heads * ((tp + distance) % NTP), heads, 0)
        kv_pieces.append(tp_shift(part, distance) if distance else part)

    ranked = vertical_keys.reshape(heads, KEPT // SLOTS, SLOTS, NCTX) - base
    own_keys = jnp.max(jnp.where((ranked >= 0) & (ranked < TOK), ranked, -1), axis=1)
    own_keys = own_keys.transpose(0, 2, 1).reshape(heads, NCTX * SLOTS, 1)
    devices = jnp.arange(NCTX, dtype=jnp.int32)
    started = jnp.sum(
        vertical_keys[:, None, :] < (devices * TOK)[None, :, None], axis=2, dtype=jnp.int32
    )
    kept_first = (started - ctx + NCTX - 1) // NCTX
    piece_rows = (tp + NTP - jnp.arange(NTP, dtype=jnp.int32)) % NTP

    x, y, core = ctx // 8, (ctx // 2) % 4, ctx % 2
    kept_spots = (vertical_keys - base).reshape(heads, KEPT, NX, NY, NCORE)
    for axis, place, size in ((2, x, NX), (3, y, NY), (4, core, NCORE)):
        turned = jnp.flip(kept_spots, axis)
        turned = jnp.concatenate((turned, turned), axis=axis)
        kept_spots = lax.dynamic_slice_in_dim(turned, size - 1 - place, size, axis)
    spots = kept_spots.transpose(0, 4, 2, 3, 1).reshape(heads, 1, NVERT)

    blocks = jnp.arange(-1, NBLK, dtype=jnp.int32) + ctx * NBLK - hops[:, :, None]
    blocks = blocks.reshape(heads, 3 * (NBLK + 1))
    high = (vertical_keys[:, :, None] // BLOCK == blocks[:, None, :]).astype(BF16)
    low = (vertical_keys[:, :, None] % BLOCK == jnp.arange(BLOCK)).astype(BF16)
    marked = jnp.einsum("hnb,hnl->hbl", high, low, preferred_element_type=F32)
    marks = jnp.where((marked > 0.5) | (blocks < 0)[:, :, None], NEG, 0.0)
    marks = marks.reshape(heads, 3, NBLK + 1, BLOCK)
    marks = jnp.concatenate((marks[:, :, :-1], marks[:, :, 1:]), axis=3)

    def query_parts(head):
        wide = GROUP * DH
        firsts = [wide * (heads * ((tp + step) % NTP) + head) for step in range(NTP)]
        return [lax.dynamic_slice_in_dim(queries, first, wide, 1) for first in firsts]

    def send_queries(parts):
        return parts[:1] + [tp_shift(parts[step], step) for step in (1, 2, 3)]

    first_parts, second_parts = query_parts(0), query_parts(1)
    received, first_parts = lax.optimization_barrier((kv_pieces[1:], first_parts))
    first_queries = send_queries(first_parts)
    local, sent = join_pieces(piece_rows, own_keys, kv_pieces[:1] + received)
    beside = ctx_next(local[:, TOK - BLOCK :])

    table = lax.all_to_all(sent, "ctx", split_axis=0, concat_axis=0, tiled=True)
    orders = far_hops % NBLK
    table, marks, spots, kept_first, orders = lax.optimization_barrier(
        (table, marks, spots, kept_first, orders)
    )

    kept = keep_verticals(kept_first, table)
    along_y = [kept] + [
        ctx_route(kept, lambda x, y, core, step=step: (x, y + step, core)) for step in (1, 2, 3)
    ]
    shifts = (ctx % NBLK + jnp.where(ctx < NBLK, far_hops[0], far_hops[1])) // NBLK
    spread = spread_windows(shifts, table)
    along_y, beside, spread = lax.optimization_barrier((along_y, beside, spread))
    along_y = jnp.stack(along_y)
    along_x = [along_y] + [
        ctx_route(along_y, lambda x, y, core, step=step: (x + step, y, core)) for step in (1, 2, 3)
    ]
    spread, along_x, first_queries, second_parts = lax.optimization_barrier(
        (spread, along_x, first_queries, second_parts)
    )
    across = [ctx_route(part, lambda x, y, core: (x, y, core + 1)) for part in along_x]
    second_queries = send_queries(second_parts)
    vert = along_x + across

    windows = lax.all_to_all(
        spread, "ctx", split_axis=0, concat_axis=0, tiled=True
    ).reshape(heads, NBLK, 2, BLOCK, 2 * DH)
    prior = near_attention(0, piece_rows, first_queries, vert, beside, local, spots, marks)
    windows, prior = lax.optimization_barrier((windows, prior))
    last = last_blocks((2 * NBLK - 1 - orders).reshape(-1) % NBLK, windows)
    halo = ctx_next(last)
    out = attend(
        1,
        piece_rows,
        orders[1],
        second_queries,
        vert,
        beside,
        local,
        windows,
        halo,
        spots,
        marks,
    )
    prior, stats, query = prior
    return far_attention(
        0, piece_rows, orders[0], query, prior, stats, windows, halo, marks, out
    )


def solution(mesh):
    in_specs = (
        P(("ctx", "tp"), None),
        P(("ctx", "tp"), None),
        P(("ctx", "tp"), None),
        P("tp", None),
        P("tp", None),
    )
    out_specs = P("ctx", "tp")
    return jax.shard_map(shards, mesh=mesh, in_specs=in_specs, out_specs=out_specs, check_vma=False)
```

```python
import functools

import jax
import jax.numpy as jnp
from jax import lax
from jax.experimental import pallas as pl
from jax.experimental.pallas import tpu as pltpu
from jax.sharding import PartitionSpec as P

HQ = 64
KVH = 8
DH = 128
NVERT = 1024
GROUP = HQ // KVH
BLOCK = 64
CAP = 96
SLOTS = 8
NX, NY, NCORE, NTP = 4, 4, 2, 4
NCTX = NX * NY * NCORE
TOK = 1024
NBLK = TOK // BLOCK
KEPT = NVERT // NCTX
PIECE = TOK // NTP
LOG2_SCALE = 1.4426950408889634 * DH**-0.5
NEG = -1e30
BF16 = jnp.bfloat16
F32 = jnp.float32
VMEM_LIMIT = 63 * 2**20 + 2**19


def params():
    return pltpu.CompilerParams(vmem_limit_bytes=VMEM_LIMIT)


def dot_t(left, right):
    return lax.dot_general(left, right, (((1,), (1,)), ((), ())), preferred_element_type=F32)


def tp_shift(block, distance):
    return lax.ppermute(block, "tp", [(i, (i + distance) % NTP) for i in range(NTP)])


def ctx_route(block, move):
    pairs = []
    for x in range(NX):
        for y in range(NY):
            for core in range(NCORE):
                to_x, to_y, to_core = move(x, y, core)
                source = (x * NY + y) * NCORE + core
                target = ((to_x % NX) * NY + to_y % NY) * NCORE + to_core % NCORE
                pairs.append((source, target))
    return lax.ppermute(block, "ctx", pairs)


def ctx_next(block):
    return lax.ppermute(block, "ctx", [(i, i + 1) for i in range(NCTX - 1)])


def join_kernel(rows_ref, keys_ref, p0, p1, p2, p3, local_ref, send_ref):
    for distance, piece in enumerate((p0, p1, p2, p3)):
        first = pl.multiple_of(rows_ref[distance] * PIECE, PIECE)
        local_ref[:, pl.ds(first, PIECE), :] = piece[...]
    spots = lax.broadcasted_iota(jnp.int32, (NCTX * SLOTS, TOK), 1)
    chosen = []
    for head in range(2):
        pick = jnp.where(keys_ref[head] == spots, 1.0, 0.0).astype(BF16)
        rows = jnp.dot(pick, local_ref[head], preferred_element_type=F32)
        chosen.append(rows.reshape(NCTX, SLOTS, 2 * DH))
        for block in range(NBLK):
            send_ref[head * NBLK + block, :BLOCK, :] = local_ref[
                head, block * BLOCK : (block + 1) * BLOCK, :
            ]
    send_ref[:, BLOCK:, :] = jnp.concatenate(chosen, axis=1).astype(BF16)


def join_pieces(rows, keys, pieces):
    vmem = pl.BlockSpec(memory_space=pltpu.VMEM)
    return pl.pallas_call(
        join_kernel,
        in_specs=[pl.BlockSpec(memory_space=pltpu.SMEM)] + [vmem] * 5,
        out_specs=[vmem, vmem],
        out_shape=[
            jax.ShapeDtypeStruct((2, TOK, 2 * DH), BF16),
            jax.ShapeDtypeStruct((NCTX, BLOCK + 2 * SLOTS, 2 * DH), BF16),
        ],
        compiler_params=params(),
    )(rows, keys, *pieces)


def last_kernel(order_ref, *refs):
    for i in range(4):
        refs[4][i // 2, i % 2] = refs[i][0, 0, 0]


def last_blocks(orders, windows):
    def block(i):
        return pl.BlockSpec((1, 1, 1, BLOCK, 2 * DH), lambda g, s: (i // 2, s[i], i % 2, 0, 0))

    return pl.pallas_call(
        last_kernel,
        grid_spec=pltpu.PrefetchScalarGridSpec(
            num_scalar_prefetch=1,
            grid=(1,),
            in_specs=[block(i) for i in range(4)],
            out_specs=pl.BlockSpec((2, 2, BLOCK, 2 * DH), lambda g, s: (0, 0, 0, 0)),
        ),
        out_shape=jax.ShapeDtypeStruct((2, 2, BLOCK, 2 * DH), BF16),
        compiler_params=params(),
    )(orders, windows, windows, windows, windows)


def keep_kernel(first_ref, rows_ref, out_ref, total):
    total[...] = jnp.zeros_like(total)
    slot = lax.broadcasted_iota(jnp.int32, (SLOTS, 2 * DH), 0)
    for source in range(NCTX):
        for head in range(2):
            first = first_ref[head, source]
            rows = rows_ref[source].astype(F32)[head * SLOTS : (head + 1) * SLOTS]
            group = pl.multiple_of(first // SLOTS * SLOTS, SLOTS)
            late = slot >= lax.rem(first, SLOTS)
            total[head, pl.ds(group, SLOTS), :] += jnp.where(late, rows, 0.0)
            total[head, pl.ds(group + SLOTS, SLOTS), :] += jnp.where(late, 0.0, rows)
    out_ref[...] = total[:, :KEPT, :].astype(BF16)


def keep_verticals(firsts, table):
    return pl.pallas_call(
        keep_kernel,
        grid_spec=pltpu.PrefetchScalarGridSpec(
            num_scalar_prefetch=1,
            grid=(1,),
            in_specs=[pl.BlockSpec((NCTX, 2 * SLOTS, 2 * DH), lambda i, s: (0, BLOCK // 16, 0))],
            out_specs=pl.BlockSpec((2, KEPT, 2 * DH), lambda i, s: (0, 0, 0)),
            scratch_shapes=[pltpu.VMEM((2, KEPT + 2 * SLOTS, 2 * DH), F32)],
        ),
        out_shape=jax.ShapeDtypeStruct((2, KEPT, 2 * DH), BF16),
        compiler_params=params(),
    )(firsts, table)


def spread_kernel(shift_ref, table_ref, out_ref):
    group = pl.program_id(0)
    for i in range(8):
        for band in range(2):
            source = jnp.maximum(group * 8 + i - shift_ref[band], 0)
            out_ref[i, band] = table_ref[source, :BLOCK, :]


def spread_windows(shifts, table):
    return pl.pallas_call(
        spread_kernel,
        grid_spec=pltpu.PrefetchScalarGridSpec(
            num_scalar_prefetch=1,
            grid=(NCTX // 8,),
            in_specs=[pl.BlockSpec(table.shape, lambda g, s: (0, 0, 0))],
            out_specs=pl.BlockSpec((8, 2, BLOCK, 2 * DH), lambda g, s: (g, 0, 0, 0)),
        ),
        out_shape=jax.ShapeDtypeStruct((NCTX, 2, BLOCK, 2 * DH), BF16),
        compiler_params=params(),
    )(shifts, table)


def stack_heads(ref, first):
    return jnp.concatenate(
        [ref[first : first + BLOCK, g * DH : (g + 1) * DH] for g in range(GROUP)], axis=0
    )


def band_bias():
    row = lax.broadcasted_iota(jnp.int32, (BLOCK, 2 * BLOCK), 0)
    column = lax.broadcasted_iota(jnp.int32, (BLOCK, 2 * BLOCK), 1)
    distance = row - column + BLOCK
    return jnp.where((distance >= 0) & (distance < BLOCK), 0.0, NEG)


def masked(scores, bias):
    width = scores.shape[1]
    return (scores.reshape(GROUP, BLOCK, width) + bias[None]).reshape(GROUP * BLOCK, width)


def pack_levels(levels):
    lanes = lax.broadcasted_iota(jnp.int32, (BLOCK, DH), 1)
    packed = jnp.zeros((BLOCK, DH), F32)
    for g in range(GROUP):
        packed = jnp.where(lanes == g, levels[g * BLOCK : (g + 1) * BLOCK], packed)
    high = packed.astype(BF16)
    rest = packed - high.astype(F32)
    middle = rest.astype(BF16)
    low = (rest - middle.astype(F32)).astype(BF16)
    terms = high.astype(F32) + pltpu.roll(middle.astype(F32), GROUP, 1)
    return (terms + pltpu.roll(low.astype(F32), 2 * GROUP, 1)).astype(BF16)


def level_picks():
    lane = lax.broadcasted_iota(jnp.int32, (DH, GROUP * DH), 0)
    head = lax.broadcasted_iota(jnp.int32, (DH, GROUP * DH), 1) // DH
    pick = (lane < 3 * GROUP) & (lane % GROUP == head)
    return jnp.where(pick, 1.0, 0.0).astype(BF16)


def spread_levels(packed, picks):
    spread = jnp.dot(packed, picks, preferred_element_type=F32)
    return jnp.concatenate([spread[:, g * DH : (g + 1) * DH] for g in range(GROUP)], axis=0)


def near_kernel(rows_ref, *refs):
    q_refs, vert_refs = refs[:NTP], refs[NTP : NTP + 8]
    beside_ref, local_ref, spot_ref, mark_ref = refs[NTP + 8 : NTP + 12]
    out_ref, stat_ref, copy_ref, vert_ref, band_ref = refs[-5:]
    piece = pl.program_id(0)
    for i in range(NTP):

        @pl.when(piece == i)
        def _():
            copy_ref[0] = q_refs[i][...]

    @pl.when(piece == 0)
    def _():
        for number, part in enumerate(vert_refs):
            for i in range(4):
                first = (number * 4 + i) * KEPT
                vert_ref[first : first + KEPT, : 2 * DH] = part[i, 0]
        vert_ref[:, 2 * DH :] = jnp.ones((NVERT, DH), BF16)
        band_ref[:BLOCK, : 2 * DH] = beside_ref[0]
        band_ref[BLOCK:, : 2 * DH] = local_ref[0]
        band_ref[:, 2 * DH :] = jnp.ones((TOK + BLOCK, DH), BF16)

    bias = band_bias()

    def score(sub):
        block = rows_ref[piece] * (PIECE // BLOCK) + sub
        query = stack_heads(copy_ref.at[0], sub * BLOCK)
        first = pl.multiple_of(block * BLOCK, BLOCK)
        near = jnp.concatenate(
            [band_ref[pl.ds(first, BLOCK), :], band_ref[pl.ds(first + BLOCK, BLOCK), :]], axis=0
        )
        return block, near, dot_t(query, vert_ref[:, :DH]), dot_t(query, near[:, :DH])

    def weigh(block, near, vert_s, near_s):
        position = block * BLOCK + lax.broadcasted_iota(jnp.int32, (BLOCK, NVERT), 0)
        vert_s = masked(vert_s, jnp.where(spot_ref[0] <= position, 0.0, NEG))
        near_s = masked(near_s, bias + mark_ref[0, 0, pl.ds(block, 1), :])
        top = near_s
        for first in range(0, NVERT, DH):
            top = jnp.maximum(top, vert_s[:, first : first + DH])
        top = jnp.max(top, axis=-1, keepdims=True) * LOG2_SCALE
        vert_w = jnp.exp2(vert_s * LOG2_SCALE - top).astype(BF16)
        near_w = jnp.exp2(near_s * LOG2_SCALE - top).astype(BF16)
        return near, top, vert_w, near_w

    def finish(sub, near, top, vert_w, near_w):
        both = jnp.dot(vert_w, vert_ref[:, DH:], preferred_element_type=F32)
        both = both + jnp.dot(
            near_w, near[:, DH:], preferred_element_type=F32
        )
        total = both[:, DH:]
        out = (both[:, :DH] / total).astype(BF16)
        rows = slice(sub * BLOCK, (sub + 1) * BLOCK)
        stat_ref[0, rows, :] = pack_levels(top + jnp.log2(total))
        for g in range(GROUP):
            out_ref[0, rows, g * DH : (g + 1) * DH] = out[g * BLOCK : (g + 1) * BLOCK]

    subtiles = PIECE // BLOCK
    scored, weighed = score(0), None
    for sub in range(subtiles):
        following = score(sub + 1) if sub + 1 < subtiles else None
        current = weigh(*scored)
        if weighed is not None:
            finish(sub - 1, *weighed)
        scored, weighed = following, current
    finish(subtiles - 1, *weighed)


def near_attention(head, rows, queries, vert, beside, local, spots, marks):
    wide = GROUP * DH
    here = lambda p, s: (p, 0, 0)
    return pl.pallas_call(
        near_kernel,
        grid_spec=pltpu.PrefetchScalarGridSpec(
            num_scalar_prefetch=1,
            grid=(NTP,),
            in_specs=[pl.BlockSpec((PIECE, wide), lambda p, s: (0, 0))] * NTP
            + [pl.BlockSpec((4, 1, KEPT, 2 * DH), lambda p, s: (0, head, 0, 0))] * 8
            + [
                pl.BlockSpec((1, BLOCK, 2 * DH), lambda p, s: (head, 0, 0)),
                pl.BlockSpec((1, TOK, 2 * DH), lambda p, s: (head, 0, 0)),
                pl.BlockSpec((1, 1, NVERT), lambda p, s: (head, 0, 0)),
                pl.BlockSpec((1, 1, NBLK, 2 * BLOCK), lambda p, s: (head, 0, 0, 0)),
            ],
            out_specs=[
                pl.BlockSpec((1, PIECE, wide), here),
                pl.BlockSpec((1, PIECE, DH), here),
                pl.BlockSpec((1, PIECE, wide), here),
            ],
            scratch_shapes=[
                pltpu.VMEM((NVERT, 3 * DH), BF16),
                pltpu.VMEM((TOK + BLOCK, 3 * DH), BF16),
            ],
        ),
        out_shape=[
            jax.ShapeDtypeStruct((NTP, PIECE, wide), BF16),
            jax.ShapeDtypeStruct((NTP, PIECE, DH), BF16),
            jax.ShapeDtypeStruct((NTP, PIECE, wide), BF16),
        ],
        cost_estimate=pl.CostEstimate(flops=10**9, bytes_accessed=2**20, transcendentals=0),
        compiler_params=params(),
    )(rows, *queries, *vert, beside, local, spots, marks)


def far_step(
    piece,
    rows_ref,
    order_ref,
    q_ref,
    prior_ref,
    stat_ref,
    far_ref,
    halo_ref,
    mark_ref,
    out_ref,
    keys,
    picks,
):
    @pl.when(piece == 0)
    def _():
        picks[...] = level_picks()
        for band in range(2):
            keys[band, :BLOCK, :] = halo_ref[0, band]
            for block in range(NBLK):
                source = lax.rem(block + NBLK - order_ref[band], NBLK)
                keys[band, (block + 1) * BLOCK : (block + 2) * BLOCK, :] = far_ref[0, source, band]

    ones = jnp.ones((4 * BLOCK, DH), BF16)
    bias = band_bias()
    for sub in range(PIECE // BLOCK):
        block = rows_ref[piece] * (PIECE // BLOCK) + sub
        first = pl.multiple_of(block * BLOCK, BLOCK)
        rows = slice(sub * BLOCK, (sub + 1) * BLOCK)
        query = stack_heads(q_ref.at[0], sub * BLOCK)
        near = jnp.concatenate([keys[band, pl.ds(first, 2 * BLOCK), :] for band in range(2)], axis=0)
        scores = dot_t(query, near[:, :DH])
        halves = [
            masked(
                scores[:, band * DH : (band + 1) * DH],
                bias + mark_ref[0, 1 + band, pl.ds(block, 1), :],
            )
            for band in range(2)
        ]
        level = spread_levels(stat_ref[0, rows, :], picks[...])
        top = jnp.max(jnp.maximum(halves[0], halves[1]), axis=-1, keepdims=True) * LOG2_SCALE
        top = jnp.maximum(top, level)
        weight = jnp.concatenate(
            [jnp.exp2(half * LOG2_SCALE - top).astype(BF16) for half in halves], axis=1
        )
        both = jnp.dot(
            weight, jnp.concatenate([near[:, DH:], ones], axis=1), preferred_element_type=F32
        )
        prior_w = jnp.exp2(level - top)
        total = both[:, DH:] + prior_w
        prior = stack_heads(prior_ref.at[0], sub * BLOCK).astype(F32)
        out = ((both[:, :DH] + prior * prior_w) / total).astype(BF16)
        for g in range(GROUP):
            out_ref[rows, g * DH : (g + 1) * DH] = out[g * BLOCK : (g + 1) * BLOCK]


def attend_step(
    piece,
    rows_ref,
    order_ref,
    q_refs,
    vert_refs,
    beside_ref,
    local_ref,
    far_ref,
    halo_ref,
    spot_ref,
    mark_ref,
    out_ref,
    query_ref,
    vert_ref,
    band_ref,
):
    for i in range(NTP):

        @pl.when(piece == i)
        def _():
            query_ref[...] = q_refs[i][...]

    @pl.when(piece == 0)
    def _():
        for number, part in enumerate(vert_refs):
            for i in range(4):
                first = (number * 4 + i) * KEPT
                vert_ref[first : first + KEPT, : 2 * DH] = part[i, 0]
        vert_ref[:, 2 * DH :] = jnp.ones((NVERT, DH), BF16)
        band_ref[2, :BLOCK, :] = beside_ref[0]
        band_ref[2, BLOCK:, :] = local_ref[0]
        for band in range(2):
            band_ref[band, :BLOCK, :] = halo_ref[0, band]
            for block in range(NBLK):
                source = lax.rem(block + NBLK - order_ref[2 + band], NBLK)
                band_ref[band, (block + 1) * BLOCK : (block + 2) * BLOCK, :] = far_ref[
                    0, source, band
                ]

    ones = jnp.ones((6 * BLOCK, DH), BF16)
    bias = band_bias()

    def score(sub):
        block = rows_ref[piece] * (PIECE // BLOCK) + sub
        query = stack_heads(query_ref, sub * BLOCK)
        window = pl.ds(pl.multiple_of(block * BLOCK, BLOCK), 2 * BLOCK)
        band = jnp.concatenate(
            [band_ref[2, window, :], band_ref[0, window, :], band_ref[1, window, :]], axis=0
        )
        return block, band, dot_t(query, vert_ref[:, :DH]), dot_t(query, band[:, :DH])

    def weigh(block, band, vert_s, band_s):
        position = block * BLOCK + lax.broadcasted_iota(jnp.int32, (BLOCK, NVERT), 0)
        vert_s = masked(vert_s, jnp.where(spot_ref[0] <= position, 0.0, NEG))
        band_bias_s = jnp.concatenate(
            [bias + mark_ref[0, i, pl.ds(block, 1), :] for i in range(3)], axis=1
        )
        band_s = masked(band_s, band_bias_s)
        top = band_s[:, :DH]
        for first in range(DH, 3 * DH, DH):
            top = jnp.maximum(top, band_s[:, first : first + DH])
        for first in range(0, NVERT, DH):
            top = jnp.maximum(top, vert_s[:, first : first + DH])
        top = jnp.max(top, axis=-1, keepdims=True) * LOG2_SCALE
        vert_w = jnp.exp2(vert_s * LOG2_SCALE - top).astype(BF16)
        band_w = jnp.exp2(band_s * LOG2_SCALE - top).astype(BF16)
        return band, vert_w, band_w

    def finish(sub, band, vert_w, band_w):
        both = jnp.dot(vert_w, vert_ref[:, DH:], preferred_element_type=F32)
        both = both + jnp.dot(
            band_w, jnp.concatenate([band[:, DH:], ones], axis=1), preferred_element_type=F32
        )
        out = (both[:, :DH] / both[:, DH:]).astype(BF16)
        rows = slice(sub * BLOCK, (sub + 1) * BLOCK)
        for g in range(GROUP):
            out_ref[rows, g * DH : (g + 1) * DH] = out[g * BLOCK : (g + 1) * BLOCK]

    subtiles = PIECE // BLOCK
    scored, weighed = score(0), None
    for sub in range(subtiles):
        following = score(sub + 1) if sub + 1 < subtiles else None
        current = weigh(*scored)
        if weighed is not None:
            finish(sub - 1, *weighed)
        scored, weighed = following, current
    finish(subtiles - 1, *weighed)


def tail_kernel(rows_ref, order_ref, *refs):
    q_refs, vert_refs = refs[:NTP], refs[NTP : NTP + 8]
    beside_ref, local_ref, far_ref, halo_ref, spot_ref, mark_ref = refs[NTP + 8 : NTP + 14]
    q_ref, prior_ref, stat_ref, out_ref = refs[NTP + 14 : NTP + 18]
    query_ref, vert_ref, band_ref, picks = refs[-4:]
    step = pl.program_id(0)

    @pl.when(step < NTP)
    def _():
        attend_step(
            step,
            rows_ref,
            order_ref,
            q_refs,
            vert_refs,
            beside_ref,
            local_ref,
            far_ref,
            halo_ref,
            spot_ref,
            mark_ref,
            out_ref,
            query_ref,
            vert_ref,
            band_ref,
        )

    @pl.when(step >= NTP)
    def _():
        far_step(
            step - NTP,
            rows_ref,
            order_ref,
            q_ref,
            prior_ref,
            stat_ref,
            far_ref,
            halo_ref,
            mark_ref,
            out_ref,
            band_ref,
            picks,
        )


def tail_attention(rows, orders, queries, vert, beside, local, far, halo, spots, marks, first):
    prior, stats, query = first
    wide = GROUP * DH
    head = lambda p: 1 - p // NTP
    later = lambda p, s, o: (jnp.maximum(p - NTP, 0), 0, 0)
    return pl.pallas_call(
        tail_kernel,
        grid_spec=pltpu.PrefetchScalarGridSpec(
            num_scalar_prefetch=2,
            grid=(2 * NTP,),
            in_specs=[pl.BlockSpec((PIECE, wide), lambda p, s, o: (0, 0))] * NTP
            + [pl.BlockSpec((4, 1, KEPT, 2 * DH), lambda p, s, o: (0, 1, 0, 0))] * 8
            + [
                pl.BlockSpec((1, BLOCK, 2 * DH), lambda p, s, o: (1, 0, 0)),
                pl.BlockSpec((1, TOK, 2 * DH), lambda p, s, o: (1, 0, 0)),
                pl.BlockSpec((1, NBLK, 2, BLOCK, 2 * DH), lambda p, s, o: (head(p), 0, 0, 0, 0)),
                pl.BlockSpec((1, 2, BLOCK, 2 * DH), lambda p, s, o: (head(p), 0, 0, 0)),
                pl.BlockSpec((1, 1, NVERT), lambda p, s, o: (1, 0, 0)),
                pl.BlockSpec((1, 3, NBLK, 2 * BLOCK), lambda p, s, o: (head(p), 0, 0, 0)),
                pl.BlockSpec((1, PIECE, wide), later),
                pl.BlockSpec((1, PIECE, wide), later),
                pl.BlockSpec((1, PIECE, DH), later),
            ],
            out_specs=pl.BlockSpec((PIECE, wide), lambda p, s, o: (s[p % NTP], head(p))),
            scratch_shapes=[
                pltpu.VMEM((PIECE, wide), BF16),
                pltpu.VMEM((NVERT, 3 * DH), BF16),
                pltpu.VMEM((3, TOK + BLOCK, 2 * DH), BF16),
                pltpu.VMEM((DH, GROUP * DH), BF16),
            ],
        ),
        out_shape=jax.ShapeDtypeStruct((TOK, 2 * wide), BF16),
        compiler_params=params(),
    )(
        rows,
        orders,
        *queries,
        *vert,
        beside,
        local,
        far,
        halo,
        spots,
        marks,
        query,
        prior,
        stats,
    )


def shards(queries, key_rows, value_rows, vertical_keys, slash_offsets):
    tp = lax.axis_index("tp")
    ctx = lax.axis_index("ctx")
    base = ctx * TOK
    heads = vertical_keys.shape[0]
    hops = slash_offsets // BLOCK
    far_hops = hops[:, 1:]

    kv = jnp.concatenate(
        (key_rows.reshape(PIECE, KVH, DH), value_rows.reshape(PIECE, KVH, DH)), axis=2
    ).transpose(1, 0, 2)
    kv_pieces = []
    for distance in range(NTP):
        part = lax.dynamic_slice_in_dim(kv, heads * ((tp + distance) % NTP), heads, 0)
        kv_pieces.append(tp_shift(part, distance) if distance else part)

    ranked = vertical_keys.reshape(heads, KEPT // SLOTS, SLOTS, NCTX) - base
    own_keys = jnp.max(jnp.where((ranked >= 0) & (ranked < TOK), ranked, -1), axis=1)
    own_keys = own_keys.transpose(0, 2, 1).reshape(heads, NCTX * SLOTS, 1)
    devices = jnp.arange(NCTX, dtype=jnp.int32)
    started = jnp.sum(
        vertical_keys[:, None, :] < (devices * TOK)[None, :, None], axis=2, dtype=jnp.int32
    )
    kept_first = (started - ctx + NCTX - 1) // NCTX
    piece_rows = (tp + NTP - jnp.arange(NTP, dtype=jnp.int32)) % NTP

    x, y, core = ctx // 8, (ctx // 2) % 4, ctx % 2
    kept_spots = (vertical_keys - base).reshape(heads, KEPT, NX, NY, NCORE)
    for axis, place, size in ((2, x, NX), (3, y, NY), (4, core, NCORE)):
        turned = jnp.flip(kept_spots, axis)
        turned = jnp.concatenate((turned, turned), axis=axis)
        kept_spots = lax.dynamic_slice_in_dim(turned, size - 1 - place, size, axis)
    spots = kept_spots.transpose(0, 4, 2, 3, 1).reshape(heads, 1, NVERT)

    blocks = jnp.arange(-1, NBLK, dtype=jnp.int32) + ctx * NBLK - hops[:, :, None]
    blocks = blocks.reshape(heads, 3 * (NBLK + 1))
    high = (vertical_keys[:, :, None] // BLOCK == blocks[:, None, :]).astype(BF16)
    low = (vertical_keys[:, :, None] % BLOCK == jnp.arange(BLOCK)).astype(BF16)
    marked = jnp.einsum("hnb,hnl->hbl", high, low, preferred_element_type=F32)
    marks = jnp.where((marked > 0.5) | (blocks < 0)[:, :, None], NEG, 0.0)
    marks = marks.reshape(heads, 3, NBLK + 1, BLOCK)
    marks = jnp.concatenate((marks[:, :, :-1], marks[:, :, 1:]), axis=3)

    def query_parts(head):
        wide = GROUP * DH
        firsts = [wide * (heads * ((tp + step) % NTP) + head) for step in range(NTP)]
        return [lax.dynamic_slice_in_dim(queries, first, wide, 1) for first in firsts]

    def send_queries(parts):
        return parts[:1] + [tp_shift(parts[step], step) for step in (1, 2, 3)]

    first_parts, second_parts = query_parts(0), query_parts(1)
    received, first_parts = lax.optimization_barrier((kv_pieces[1:], first_parts))
    first_queries = send_queries(first_parts)
    local, sent = join_pieces(piece_rows, own_keys, kv_pieces[:1] + received)
    beside = ctx_next(local[:, TOK - BLOCK :])

    table = lax.all_to_all(sent, "ctx", split_axis=0, concat_axis=0, tiled=True)
    orders = far_hops % NBLK
    table, marks, spots, kept_first, orders = lax.optimization_barrier(
        (table, marks, spots, kept_first, orders)
    )

    kept = keep_verticals(kept_first, table)
    along_y = [kept] + [
        ctx_route(kept, lambda x, y, core, step=step: (x, y + step, core)) for step in (1, 2, 3)
    ]
    shifts = (ctx % NBLK + jnp.where(ctx < NBLK, far_hops[0], far_hops[1])) // NBLK
    spread = spread_windows(shifts, table)
    along_y, beside, spread = lax.optimization_barrier((along_y, beside, spread))
    along_y = jnp.stack(along_y)
    along_x = [along_y] + [
        ctx_route(along_y, lambda x, y, core, step=step: (x + step, y, core)) for step in (1, 2, 3)
    ]
    spread, along_x, first_queries, second_parts = lax.optimization_barrier(
        (spread, along_x, first_queries, second_parts)
    )
    across = [ctx_route(part, lambda x, y, core: (x, y, core + 1)) for part in along_x]
    second_queries = send_queries(second_parts)
    vert = along_x + across

    windows = lax.all_to_all(
        spread, "ctx", split_axis=0, concat_axis=0, tiled=True
    ).reshape(heads, NBLK, 2, BLOCK, 2 * DH)
    prior = near_attention(0, piece_rows, first_queries, vert, beside, local, spots, marks)
    windows, prior = lax.optimization_barrier((windows, prior))
    last = last_blocks((2 * NBLK - 1 - orders).reshape(-1) % NBLK, windows)
    halo = ctx_next(last)
    return tail_attention(
        piece_rows,
        orders.reshape(-1),
        second_queries,
        vert,
        beside,
        local,
        windows,
        halo,
        spots,
        marks,
        prior,
    )


def solution(mesh):
    in_specs = (
        P(("ctx", "tp"), None),
        P(("ctx", "tp"), None),
        P(("ctx", "tp"), None),
        P("tp", None),
        P("tp", None),
    )
    out_specs = P("ctx", "tp")
    return jax.shard_map(shards, mesh=mesh, in_specs=in_specs, out_specs=out_specs, check_vma=False)
```

```python
import functools

import jax
import jax.numpy as jnp
from jax import lax
from jax.experimental import pallas as pl
from jax.experimental.pallas import tpu as pltpu
from jax.sharding import PartitionSpec as P

HQ = 64
KVH = 8
DH = 128
NVERT = 1024
GROUP = HQ // KVH
BLOCK = 64
CAP = 96
SLOTS = 8
NX, NY, NCORE, NTP = 4, 4, 2, 4
NCTX = NX * NY * NCORE
TOK = 1024
NBLK = TOK // BLOCK
KEPT = NVERT // NCTX
PIECE = TOK // NTP
LOG2_SCALE = 1.4426950408889634 * DH**-0.5
NEG = -1e30
BF16 = jnp.bfloat16
F32 = jnp.float32
VMEM_LIMIT = 63 * 2**20 + 2**19


def params():
    return pltpu.CompilerParams(vmem_limit_bytes=VMEM_LIMIT)


def dot_t(left, right):
    return lax.dot_general(left, right, (((1,), (1,)), ((), ())), preferred_element_type=F32)


def tp_shift(block, distance):
    return lax.ppermute(block, "tp", [(i, (i + distance) % NTP) for i in range(NTP)])


def ctx_route(block, move):
    pairs = []
    for x in range(NX):
        for y in range(NY):
            for core in range(NCORE):
                to_x, to_y, to_core = move(x, y, core)
                source = (x * NY + y) * NCORE + core
                target = ((to_x % NX) * NY + to_y % NY) * NCORE + to_core % NCORE
                pairs.append((source, target))
    return lax.ppermute(block, "ctx", pairs)


def ctx_next(block):
    return lax.ppermute(block, "ctx", [(i, i + 1) for i in range(NCTX - 1)])


def join_kernel(rows_ref, keys_ref, p0, p1, p2, p3, local_ref, send_ref):
    for distance, piece in enumerate((p0, p1, p2, p3)):
        first = pl.multiple_of(rows_ref[distance] * PIECE, PIECE)
        local_ref[:, pl.ds(first, PIECE), :] = piece[...]
    spots = lax.broadcasted_iota(jnp.int32, (NCTX * SLOTS, TOK), 1)
    chosen = []
    for head in range(2):
        pick = jnp.where(keys_ref[head] == spots, 1.0, 0.0).astype(BF16)
        rows = jnp.dot(pick, local_ref[head], preferred_element_type=F32)
        chosen.append(rows.reshape(NCTX, SLOTS, 2 * DH))
        for block in range(NBLK):
            send_ref[head * NBLK + block, :BLOCK, :] = local_ref[
                head, block * BLOCK : (block + 1) * BLOCK, :
            ]
    send_ref[:, BLOCK:, :] = jnp.concatenate(chosen, axis=1).astype(BF16)


def join_pieces(rows, keys, pieces):
    vmem = pl.BlockSpec(memory_space=pltpu.VMEM)
    return pl.pallas_call(
        join_kernel,
        in_specs=[pl.BlockSpec(memory_space=pltpu.SMEM)] + [vmem] * 5,
        out_specs=[vmem, vmem],
        out_shape=[
            jax.ShapeDtypeStruct((2, TOK, 2 * DH), BF16),
            jax.ShapeDtypeStruct((NCTX, BLOCK + 2 * SLOTS, 2 * DH), BF16),
        ],
        compiler_params=params(),
    )(rows, keys, *pieces)


def last_kernel(order_ref, *refs):
    for i in range(4):
        refs[4][i // 2, i % 2] = refs[i][0, 0, 0]


def last_blocks(orders, windows):
    def block(i):
        return pl.BlockSpec((1, 1, 1, BLOCK, 2 * DH), lambda g, s: (i // 2, s[i], i % 2, 0, 0))

    return pl.pallas_call(
        last_kernel,
        grid_spec=pltpu.PrefetchScalarGridSpec(
            num_scalar_prefetch=1,
            grid=(1,),
            in_specs=[block(i) for i in range(4)],
            out_specs=pl.BlockSpec((2, 2, BLOCK, 2 * DH), lambda g, s: (0, 0, 0, 0)),
        ),
        out_shape=jax.ShapeDtypeStruct((2, 2, BLOCK, 2 * DH), BF16),
        compiler_params=params(),
    )(orders, windows, windows, windows, windows)


def keep_kernel(first_ref, rows_ref, out_ref, total):
    total[...] = jnp.zeros_like(total)
    slot = lax.broadcasted_iota(jnp.int32, (SLOTS, 2 * DH), 0)
    for source in range(NCTX):
        for head in range(2):
            first = first_ref[head, source]
            rows = rows_ref[source].astype(F32)[head * SLOTS : (head + 1) * SLOTS]
            group = pl.multiple_of(first // SLOTS * SLOTS, SLOTS)
            late = slot >= lax.rem(first, SLOTS)
            total[head, pl.ds(group, SLOTS), :] += jnp.where(late, rows, 0.0)
            total[head, pl.ds(group + SLOTS, SLOTS), :] += jnp.where(late, 0.0, rows)
    out_ref[...] = total[:, :KEPT, :].astype(BF16)


def keep_verticals(firsts, table):
    return pl.pallas_call(
        keep_kernel,
        grid_spec=pltpu.PrefetchScalarGridSpec(
            num_scalar_prefetch=1,
            grid=(1,),
            in_specs=[pl.BlockSpec((NCTX, 2 * SLOTS, 2 * DH), lambda i, s: (0, BLOCK // 16, 0))],
            out_specs=pl.BlockSpec((2, KEPT, 2 * DH), lambda i, s: (0, 0, 0)),
            scratch_shapes=[pltpu.VMEM((2, KEPT + 2 * SLOTS, 2 * DH), F32)],
        ),
        out_shape=jax.ShapeDtypeStruct((2, KEPT, 2 * DH), BF16),
        compiler_params=params(),
    )(firsts, table)


def spread_kernel(shift_ref, table_ref, out_ref):
    group = pl.program_id(0)
    for i in range(8):
        for band in range(2):
            source = jnp.maximum(group * 8 + i - shift_ref[band], 0)
            out_ref[i, band] = table_ref[source, :BLOCK, :]


def spread_windows(shifts, table):
    return pl.pallas_call(
        spread_kernel,
        grid_spec=pltpu.PrefetchScalarGridSpec(
            num_scalar_prefetch=1,
            grid=(NCTX // 8,),
            in_specs=[pl.BlockSpec(table.shape, lambda g, s: (0, 0, 0))],
            out_specs=pl.BlockSpec((8, 2, BLOCK, 2 * DH), lambda g, s: (g, 0, 0, 0)),
        ),
        out_shape=jax.ShapeDtypeStruct((NCTX, 2, BLOCK, 2 * DH), BF16),
        compiler_params=params(),
    )(shifts, table)


def stack_heads(ref, first):
    return jnp.concatenate(
        [ref[first : first + BLOCK, g * DH : (g + 1) * DH] for g in range(GROUP)], axis=0
    )


def band_bias():
    row = lax.broadcasted_iota(jnp.int32, (BLOCK, 2 * BLOCK), 0)
    column = lax.broadcasted_iota(jnp.int32, (BLOCK, 2 * BLOCK), 1)
    distance = row - column + BLOCK
    return jnp.where((distance >= 0) & (distance < BLOCK), 0.0, NEG)


def masked(scores, bias):
    width = scores.shape[1]
    return (scores.reshape(GROUP, BLOCK, width) + bias[None]).reshape(GROUP * BLOCK, width)


def pack_levels(levels):
    lanes = lax.broadcasted_iota(jnp.int32, (BLOCK, DH), 1)
    packed = jnp.zeros((BLOCK, DH), F32)
    for g in range(GROUP):
        packed = jnp.where(lanes == g, levels[g * BLOCK : (g + 1) * BLOCK], packed)
    high = packed.astype(BF16)
    rest = packed - high.astype(F32)
    middle = rest.astype(BF16)
    low = (rest - middle.astype(F32)).astype(BF16)
    terms = high.astype(F32) + pltpu.roll(middle.astype(F32), GROUP, 1)
    return (terms + pltpu.roll(low.astype(F32), 2 * GROUP, 1)).astype(BF16)


def level_picks():
    lane = lax.broadcasted_iota(jnp.int32, (DH, GROUP * DH), 0)
    head = lax.broadcasted_iota(jnp.int32, (DH, GROUP * DH), 1) // DH
    pick = (lane < 3 * GROUP) & (lane % GROUP == head)
    return jnp.where(pick, 1.0, 0.0).astype(BF16)


def spread_levels(packed, picks):
    spread = jnp.dot(packed, picks, preferred_element_type=F32)
    return jnp.concatenate([spread[:, g * DH : (g + 1) * DH] for g in range(GROUP)], axis=0)


def near_kernel(rows_ref, *refs):
    q_refs, vert_refs = refs[:NTP], refs[NTP : NTP + 8]
    beside_ref, local_ref, spot_ref, mark_ref = refs[NTP + 8 : NTP + 12]
    out_ref, stat_ref, copy_ref, vert_ref, band_ref = refs[-5:]
    piece = pl.program_id(0)
    for i in range(NTP):

        @pl.when(piece == i)
        def _():
            copy_ref[0] = q_refs[i][...]

    @pl.when(piece == 0)
    def _():
        for number, part in enumerate(vert_refs):
            for i in range(4):
                first = (number * 4 + i) * KEPT
                vert_ref[first : first + KEPT, : 2 * DH] = part[i, 0]
        vert_ref[:, 2 * DH :] = jnp.ones((NVERT, DH), BF16)
        band_ref[:BLOCK, : 2 * DH] = beside_ref[0]
        band_ref[BLOCK:, : 2 * DH] = local_ref[0]
        band_ref[:, 2 * DH :] = jnp.ones((TOK + BLOCK, DH), BF16)

    bias = band_bias()

    def score(sub):
        block = rows_ref[piece] * (PIECE // BLOCK) + sub
        query = stack_heads(copy_ref.at[0], sub * BLOCK)
        first = pl.multiple_of(block * BLOCK, BLOCK)
        near = jnp.concatenate(
            [band_ref[pl.ds(first, BLOCK), :], band_ref[pl.ds(first + BLOCK, BLOCK), :]], axis=0
        )
        return block, near, dot_t(query, vert_ref[:, :DH]), dot_t(query, near[:, :DH])

    def weigh(block, near, vert_s, near_s):
        position = block * BLOCK + lax.broadcasted_iota(jnp.int32, (BLOCK, NVERT), 0)
        vert_s = masked(vert_s, jnp.where(spot_ref[0] <= position, 0.0, NEG))
        near_s = masked(near_s, bias + mark_ref[0, 0, pl.ds(block, 1), :])
        top = near_s
        for first in range(0, NVERT, DH):
            top = jnp.maximum(top, vert_s[:, first : first + DH])
        top = jnp.max(top, axis=-1, keepdims=True) * LOG2_SCALE
        vert_w = jnp.exp2(vert_s * LOG2_SCALE - top).astype(BF16)
        near_w = jnp.exp2(near_s * LOG2_SCALE - top).astype(BF16)
        return near, top, vert_w, near_w

    def finish(sub, near, top, vert_w, near_w):
        both = jnp.dot(vert_w, vert_ref[:, DH:], preferred_element_type=F32)
        both = both + jnp.dot(
            near_w, near[:, DH:], preferred_element_type=F32
        )
        total = both[:, DH:]
        out = (both[:, :DH] / total).astype(BF16)
        rows = slice(sub * BLOCK, (sub + 1) * BLOCK)
        stat_ref[0, rows, :] = pack_levels(top + jnp.log2(total))
        for g in range(GROUP):
            out_ref[0, rows, g * DH : (g + 1) * DH] = out[g * BLOCK : (g + 1) * BLOCK]

    subtiles = PIECE // BLOCK
    scored, weighed = score(0), None
    for sub in range(subtiles):
        following = score(sub + 1) if sub + 1 < subtiles else None
        current = weigh(*scored)
        if weighed is not None:
            finish(sub - 1, *weighed)
        scored, weighed = following, current
    finish(subtiles - 1, *weighed)


def near_attention(head, rows, queries, vert, beside, local, spots, marks):
    wide = GROUP * DH
    here = lambda p, s: (p, 0, 0)
    return pl.pallas_call(
        near_kernel,
        grid_spec=pltpu.PrefetchScalarGridSpec(
            num_scalar_prefetch=1,
            grid=(NTP,),
            in_specs=[pl.BlockSpec((PIECE, wide), lambda p, s: (0, 0))] * NTP
            + [
                pl.BlockSpec((4, 1, KEPT, 2 * DH), lambda p, s, i=i: (i, head, 0, 0))
                for i in (0, 0, 0, 0, 0, 1, 2, 3)
            ]
            + [
                pl.BlockSpec((1, BLOCK, 2 * DH), lambda p, s: (head, 0, 0)),
                pl.BlockSpec((1, TOK, 2 * DH), lambda p, s: (head, 0, 0)),
                pl.BlockSpec((1, 1, NVERT), lambda p, s: (head, 0, 0)),
                pl.BlockSpec((1, 1, NBLK, 2 * BLOCK), lambda p, s: (head, 0, 0, 0)),
            ],
            out_specs=[
                pl.BlockSpec((1, PIECE, wide), here),
                pl.BlockSpec((1, PIECE, DH), here),
                pl.BlockSpec((1, PIECE, wide), here),
            ],
            scratch_shapes=[
                pltpu.VMEM((NVERT, 3 * DH), BF16),
                pltpu.VMEM((TOK + BLOCK, 3 * DH), BF16),
            ],
        ),
        out_shape=[
            jax.ShapeDtypeStruct((NTP, PIECE, wide), BF16),
            jax.ShapeDtypeStruct((NTP, PIECE, DH), BF16),
            jax.ShapeDtypeStruct((NTP, PIECE, wide), BF16),
        ],
        cost_estimate=pl.CostEstimate(flops=10**9, bytes_accessed=2**20, transcendentals=0),
        compiler_params=params(),
    )(rows, *queries, *vert, beside, local, spots, marks)


def far_step(
    piece,
    rows_ref,
    order_ref,
    q_ref,
    prior_ref,
    stat_ref,
    far_ref,
    halo_ref,
    mark_ref,
    out_ref,
    keys,
    picks,
):
    @pl.when(piece == 0)
    def _():
        picks[...] = level_picks()
        for band in range(2):
            keys[band, :BLOCK, :] = halo_ref[0, band]
            for block in range(NBLK):
                source = lax.rem(block + NBLK - order_ref[band], NBLK)
                keys[band, (block + 1) * BLOCK : (block + 2) * BLOCK, :] = far_ref[0, source, band]

    ones = jnp.ones((4 * BLOCK, DH), BF16)
    bias = band_bias()
    for sub in range(PIECE // BLOCK):
        block = rows_ref[piece] * (PIECE // BLOCK) + sub
        first = pl.multiple_of(block * BLOCK, BLOCK)
        rows = slice(sub * BLOCK, (sub + 1) * BLOCK)
        query = stack_heads(q_ref.at[0], sub * BLOCK)
        near = jnp.concatenate([keys[band, pl.ds(first, 2 * BLOCK), :] for band in range(2)], axis=0)
        scores = dot_t(query, near[:, :DH])
        halves = [
            masked(
                scores[:, band * DH : (band + 1) * DH],
                bias + mark_ref[0, 1 + band, pl.ds(block, 1), :],
            )
            for band in range(2)
        ]
        level = spread_levels(stat_ref[0, rows, :], picks[...])
        top = jnp.max(jnp.maximum(halves[0], halves[1]), axis=-1, keepdims=True) * LOG2_SCALE
        top = jnp.maximum(top, level)
        weight = jnp.concatenate(
            [jnp.exp2(half * LOG2_SCALE - top).astype(BF16) for half in halves], axis=1
        )
        both = jnp.dot(
            weight, jnp.concatenate([near[:, DH:], ones], axis=1), preferred_element_type=F32
        )
        prior_w = jnp.exp2(level - top)
        total = both[:, DH:] + prior_w
        prior = stack_heads(prior_ref.at[0], sub * BLOCK).astype(F32)
        out = ((both[:, :DH] + prior * prior_w) / total).astype(BF16)
        for g in range(GROUP):
            out_ref[rows, g * DH : (g + 1) * DH] = out[g * BLOCK : (g + 1) * BLOCK]


def attend_step(
    piece,
    rows_ref,
    order_ref,
    q_refs,
    vert_refs,
    beside_ref,
    local_ref,
    far_ref,
    halo_ref,
    spot_ref,
    mark_ref,
    out_ref,
    query_ref,
    vert_ref,
    band_ref,
):
    for i in range(NTP):

        @pl.when(piece == i)
        def _():
            query_ref[...] = q_refs[i][...]

    @pl.when(piece == 0)
    def _():
        for number, part in enumerate(vert_refs):
            for i in range(4):
                first = (number * 4 + i) * KEPT
                vert_ref[first : first + KEPT, : 2 * DH] = part[i, 0]
        vert_ref[:, 2 * DH :] = jnp.ones((NVERT, DH), BF16)
        band_ref[2, :BLOCK, :] = beside_ref[0]
        band_ref[2, BLOCK:, :] = local_ref[0]
        for band in range(2):
            band_ref[band, :BLOCK, :] = halo_ref[0, band]
            for block in range(NBLK):
                source = lax.rem(block + NBLK - order_ref[2 + band], NBLK)
                band_ref[band, (block + 1) * BLOCK : (block + 2) * BLOCK, :] = far_ref[
                    0, source, band
                ]

    ones = jnp.ones((6 * BLOCK, DH), BF16)
    bias = band_bias()

    def score(sub):
        block = rows_ref[piece] * (PIECE // BLOCK) + sub
        query = stack_heads(query_ref, sub * BLOCK)
        window = pl.ds(pl.multiple_of(block * BLOCK, BLOCK), 2 * BLOCK)
        band = jnp.concatenate(
            [band_ref[2, window, :], band_ref[0, window, :], band_ref[1, window, :]], axis=0
        )
        return block, band, dot_t(query, vert_ref[:, :DH]), dot_t(query, band[:, :DH])

    def weigh(block, band, vert_s, band_s):
        position = block * BLOCK + lax.broadcasted_iota(jnp.int32, (BLOCK, NVERT), 0)
        vert_s = masked(vert_s, jnp.where(spot_ref[0] <= position, 0.0, NEG))
        band_bias_s = jnp.concatenate(
            [bias + mark_ref[0, i, pl.ds(block, 1), :] for i in range(3)], axis=1
        )
        band_s = masked(band_s, band_bias_s)
        top = band_s[:, :DH]
        for first in range(DH, 3 * DH, DH):
            top = jnp.maximum(top, band_s[:, first : first + DH])
        for first in range(0, NVERT, DH):
            top = jnp.maximum(top, vert_s[:, first : first + DH])
        top = jnp.max(top, axis=-1, keepdims=True) * LOG2_SCALE
        vert_w = jnp.exp2(vert_s * LOG2_SCALE - top).astype(BF16)
        band_w = jnp.exp2(band_s * LOG2_SCALE - top).astype(BF16)
        return band, vert_w, band_w

    def finish(sub, band, vert_w, band_w):
        both = jnp.dot(vert_w, vert_ref[:, DH:], preferred_element_type=F32)
        both = both + jnp.dot(
            band_w, jnp.concatenate([band[:, DH:], ones], axis=1), preferred_element_type=F32
        )
        out = (both[:, :DH] / both[:, DH:]).astype(BF16)
        rows = slice(sub * BLOCK, (sub + 1) * BLOCK)
        for g in range(GROUP):
            out_ref[rows, g * DH : (g + 1) * DH] = out[g * BLOCK : (g + 1) * BLOCK]

    subtiles = PIECE // BLOCK
    scored, weighed = score(0), None
    for sub in range(subtiles):
        following = score(sub + 1) if sub + 1 < subtiles else None
        current = weigh(*scored)
        if weighed is not None:
            finish(sub - 1, *weighed)
        scored, weighed = following, current
    finish(subtiles - 1, *weighed)


def tail_kernel(rows_ref, order_ref, *refs):
    q_refs, vert_refs = refs[:NTP], refs[NTP : NTP + 8]
    beside_ref, local_ref, far_ref, halo_ref, spot_ref, mark_ref = refs[NTP + 8 : NTP + 14]
    q_ref, prior_ref, stat_ref, out_ref = refs[NTP + 14 : NTP + 18]
    query_ref, vert_ref, band_ref, picks = refs[-4:]
    step = pl.program_id(0)

    @pl.when(step < NTP)
    def _():
        attend_step(
            step,
            rows_ref,
            order_ref,
            q_refs,
            vert_refs,
            beside_ref,
            local_ref,
            far_ref,
            halo_ref,
            spot_ref,
            mark_ref,
            out_ref,
            query_ref,
            vert_ref,
            band_ref,
        )

    @pl.when(step >= NTP)
    def _():
        far_step(
            step - NTP,
            rows_ref,
            order_ref,
            q_ref,
            prior_ref,
            stat_ref,
            far_ref,
            halo_ref,
            mark_ref,
            out_ref,
            band_ref,
            picks,
        )


def tail_attention(rows, orders, queries, vert, beside, local, far, halo, spots, marks, first):
    prior, stats, query = first
    wide = GROUP * DH
    head = lambda p: 1 - p // NTP
    later = lambda p, s, o: (jnp.maximum(p - NTP, 0), 0, 0)
    return pl.pallas_call(
        tail_kernel,
        grid_spec=pltpu.PrefetchScalarGridSpec(
            num_scalar_prefetch=2,
            grid=(2 * NTP,),
            in_specs=[pl.BlockSpec((PIECE, wide), lambda p, s, o: (0, 0))] * NTP
            + [
                pl.BlockSpec((4, 1, KEPT, 2 * DH), lambda p, s, o, i=i: (i, 1, 0, 0))
                for i in (0, 0, 0, 0, 0, 1, 2, 3)
            ]
            + [
                pl.BlockSpec((1, BLOCK, 2 * DH), lambda p, s, o: (1, 0, 0)),
                pl.BlockSpec((1, TOK, 2 * DH), lambda p, s, o: (1, 0, 0)),
                pl.BlockSpec((1, NBLK, 2, BLOCK, 2 * DH), lambda p, s, o: (head(p), 0, 0, 0, 0)),
                pl.BlockSpec((1, 2, BLOCK, 2 * DH), lambda p, s, o: (head(p), 0, 0, 0)),
                pl.BlockSpec((1, 1, NVERT), lambda p, s, o: (1, 0, 0)),
                pl.BlockSpec((1, 3, NBLK, 2 * BLOCK), lambda p, s, o: (head(p), 0, 0, 0)),
                pl.BlockSpec((1, PIECE, wide), later),
                pl.BlockSpec((1, PIECE, wide), later),
                pl.BlockSpec((1, PIECE, DH), later),
            ],
            out_specs=pl.BlockSpec((PIECE, wide), lambda p, s, o: (s[p % NTP], head(p))),
            scratch_shapes=[
                pltpu.VMEM((PIECE, wide), BF16),
                pltpu.VMEM((NVERT, 3 * DH), BF16),
                pltpu.VMEM((3, TOK + BLOCK, 2 * DH), BF16),
                pltpu.VMEM((DH, GROUP * DH), BF16),
            ],
        ),
        out_shape=jax.ShapeDtypeStruct((TOK, 2 * wide), BF16),
        compiler_params=params(),
    )(
        rows,
        orders,
        *queries,
        *vert,
        beside,
        local,
        far,
        halo,
        spots,
        marks,
        query,
        prior,
        stats,
    )


def shards(queries, key_rows, value_rows, vertical_keys, slash_offsets):
    tp = lax.axis_index("tp")
    ctx = lax.axis_index("ctx")
    base = ctx * TOK
    heads = vertical_keys.shape[0]
    hops = slash_offsets // BLOCK
    far_hops = hops[:, 1:]

    kv = jnp.concatenate(
        (key_rows.reshape(PIECE, KVH, DH), value_rows.reshape(PIECE, KVH, DH)), axis=2
    ).transpose(1, 0, 2)
    kv_pieces = []
    for distance in range(NTP):
        part = lax.dynamic_slice_in_dim(kv, heads * ((tp + distance) % NTP), heads, 0)
        kv_pieces.append(tp_shift(part, distance) if distance else part)

    ranked = vertical_keys.reshape(heads, KEPT // SLOTS, SLOTS, NCTX) - base
    own_keys = jnp.max(jnp.where((ranked >= 0) & (ranked < TOK), ranked, -1), axis=1)
    own_keys = own_keys.transpose(0, 2, 1).reshape(heads, NCTX * SLOTS, 1)
    devices = jnp.arange(NCTX, dtype=jnp.int32)
    started = jnp.sum(
        vertical_keys[:, None, :] < (devices * TOK)[None, :, None], axis=2, dtype=jnp.int32
    )
    kept_first = (started - ctx + NCTX - 1) // NCTX
    piece_rows = (tp + NTP - jnp.arange(NTP, dtype=jnp.int32)) % NTP

    x, y, core = ctx // 8, (ctx // 2) % 4, ctx % 2
    kept_spots = (vertical_keys - base).reshape(heads, KEPT, NX, NY, NCORE)
    for axis, place, size in ((2, x, NX), (3, y, NY), (4, core, NCORE)):
        turned = jnp.flip(kept_spots, axis)
        turned = jnp.concatenate((turned, turned), axis=axis)
        kept_spots = lax.dynamic_slice_in_dim(turned, size - 1 - place, size, axis)
    spots = kept_spots.transpose(0, 4, 2, 3, 1).reshape(heads, 1, NVERT)

    blocks = jnp.arange(-1, NBLK, dtype=jnp.int32) + ctx * NBLK - hops[:, :, None]
    blocks = blocks.reshape(heads, 3 * (NBLK + 1))
    high = (vertical_keys[:, :, None] // BLOCK == blocks[:, None, :]).astype(BF16)
    low = (vertical_keys[:, :, None] % BLOCK == jnp.arange(BLOCK)).astype(BF16)
    marked = jnp.einsum("hnb,hnl->hbl", high, low, preferred_element_type=F32)
    marks = jnp.where((marked > 0.5) | (blocks < 0)[:, :, None], NEG, 0.0)
    marks = marks.reshape(heads, 3, NBLK + 1, BLOCK)
    marks = jnp.concatenate((marks[:, :, :-1], marks[:, :, 1:]), axis=3)

    def query_parts(head):
        wide = GROUP * DH
        firsts = [wide * (heads * ((tp + step) % NTP) + head) for step in range(NTP)]
        return [lax.dynamic_slice_in_dim(queries, first, wide, 1) for first in firsts]

    def send_queries(parts):
        return parts[:1] + [tp_shift(parts[step], step) for step in (1, 2, 3)]

    first_parts, second_parts = query_parts(0), query_parts(1)
    received, first_parts = lax.optimization_barrier((kv_pieces[1:], first_parts))
    first_queries = send_queries(first_parts)
    local, sent = join_pieces(piece_rows, own_keys, kv_pieces[:1] + received)
    beside = ctx_next(local[:, TOK - BLOCK :])

    table = lax.all_to_all(sent, "ctx", split_axis=0, concat_axis=0, tiled=True)
    orders = far_hops % NBLK
    table, marks, spots, kept_first, orders = lax.optimization_barrier(
        (table, marks, spots, kept_first, orders)
    )

    kept = keep_verticals(kept_first, table)
    along_y = [kept] + [
        ctx_route(kept, lambda x, y, core, step=step: (x, y + step, core)) for step in (1, 2, 3)
    ]
    shifts = (ctx % NBLK + jnp.where(ctx < NBLK, far_hops[0], far_hops[1])) // NBLK
    spread = spread_windows(shifts, table)
    along_y, beside, spread = lax.optimization_barrier((along_y, beside, spread))
    along_y = jnp.stack(along_y)
    along_x = [along_y] + [
        ctx_route(along_y, lambda x, y, core, step=step: (x + step, y, core)) for step in (1, 2, 3)
    ]
    spread, along_x, first_queries, second_parts = lax.optimization_barrier(
        (spread, along_x, first_queries, second_parts)
    )
    across = ctx_route(jnp.concatenate(along_x), lambda x, y, core: (x, y, core + 1))
    second_queries = send_queries(second_parts)
    vert = along_x + [across] * 4

    windows = lax.all_to_all(
        spread, "ctx", split_axis=0, concat_axis=0, tiled=True
    ).reshape(heads, NBLK, 2, BLOCK, 2 * DH)
    prior = near_attention(0, piece_rows, first_queries, vert, beside, local, spots, marks)
    windows, prior = lax.optimization_barrier((windows, prior))
    last = last_blocks((2 * NBLK - 1 - orders).reshape(-1) % NBLK, windows)
    halo = ctx_next(last)
    return tail_attention(
        piece_rows,
        orders.reshape(-1),
        second_queries,
        vert,
        beside,
        local,
        windows,
        halo,
        spots,
        marks,
        prior,
    )


def solution(mesh):
    in_specs = (
        P(("ctx", "tp"), None),
        P(("ctx", "tp"), None),
        P(("ctx", "tp"), None),
        P("tp", None),
        P("tp", None),
    )
    out_specs = P("ctx", "tp")
    return jax.shard_map(shards, mesh=mesh, in_specs=in_specs, out_specs=out_specs, check_vma=False)
```
